128 devices in a mesh: gx: 16 (over x, z), gy: 8 (over y, core).
Axes of the slice: x: 4, y: 4, z: 4, core: 2. Of those that a mesh axis runs over, the one named last changes fastest.
Arguments:
- old_state: float32 [256, 13, 16384], P(('gx', 'gy')), may hold values from -4 to 4, as said below
- new_owner: int32 [256], P(('gx', 'gy')), may hold values from 0 to 127, as said below
- new_slot: int32 [256], P(('gx', 'gy')), may hold values from 0 to 1, as said below
- neighbours: int32 [256, 6], P(('gx', 'gy')), may hold values from -1 to 1, as said below
- diffusivity: float32 [13], replicated, may hold values from 0.01 to 0.06
- stoichiometry: float32 [9], replicated, may hold values from -1 to 1
- heat_release: float32 [1], replicated, may hold values from 0.5 to 2
- prefactor: float32 [1], replicated, may hold values from 0.02 to 0.1
- activation: float32 [1], replicated, may hold values from 1 to 3
Outputs:
- final_state: float32 [256, 13, 16384], P(('gx', 'gy'))
The draws below stay inside these ranges and needn't reach their ends.
Inputs may be any that keep to these rules, and one draw needn't show every extreme that they name: `old_state`: species within 0 to 1, velocity within -4 to 4, temperature within 1 to 3. `new_owner`: devices are numbered gx index times 8 plus gy index. A box's new owner differs from its old owner in at most one of the two indices. Of one device's boxes at most one goes to a device with another gx index and at most one to a device with another gy index; both bounds are reached in every draw. Every device owns 2 boxes afterwards. The pairs (new_owner, new_slot) name every slot of every device once. The x neighbours of a box on device (i, j) are on devices ((i - 1) mod 16, j) and ((i + 1) mod 16, j), its y neighbours on (i, (j - 1) mod 8) and (i, (j + 1) mod 8), its z neighbours on the same device; -1 marks the boundary of the domain and stands only in the z columns. The relation is symmetric.
All inputs are finite; a program needn't handle non-finite values.
Results may differ from the reference program's by a relative error of at most 0.00005.
Values sent between devices are 32-bit elements; how exact they have to be, the bound alone decides.
No kernel may reach another device: no remote copies, remote signals or barrier semaphores. Data moves between devices by JAX's collectives and lax.ppermute only.
A program may use at most 192 MiB of HBM per device.

```python
import math
import jax
import jax.numpy as jnp
from jax import lax

NSPEC = 9
COMPS = 13
BX = 32
BZ = 16
BOX_CELL_TOTAL = 16384
SLOTS = 2
STEPS = 3
N_GX = 16
N_GY = 8


def random_order(key, row_count, width_count):
    scores = jax.random.randint(key, (row_count, width_count), 0, 1 << 16) * width_count
    scores = scores + jnp.arange(width_count, dtype=jnp.int32)[None, :]
    return jnp.argsort(scores, axis=1).astype(jnp.int32)


def cycle_targets(key, cycle_count, length):
    order_keys = jax.random.split(key, 2)
    orders = random_order(order_keys[0], cycle_count, length)
    successor = jnp.roll(orders, -1, axis=1)
    lines = jnp.arange(cycle_count, dtype=jnp.int32)[:, None]
    targets = jnp.zeros((cycle_count, length), jnp.int32).at[lines, orders].set(successor)
    active = jax.random.randint(order_keys[1], (cycle_count,), 0, 2).at[0].set(1)
    identity = jnp.arange(length, dtype=jnp.int32)[None, :]
    return jnp.where(active[:, None] > 0, targets, identity)


def regrid_tables(key):
    split_random_keys = jax.random.split(key, 4)
    device_count = N_GX * N_GY
    along_x = cycle_targets(split_random_keys[0], N_GY, N_GX)
    along_y = cycle_targets(split_random_keys[1], N_GX, N_GY)
    movers = random_order(split_random_keys[2], device_count, SLOTS)
    arrival = random_order(split_random_keys[3], device_count, SLOTS)
    device_ids = jnp.arange(device_count, dtype=jnp.int32)
    gx_ids = device_ids // N_GY
    gy_ids = device_ids % N_GY
    slot_ids = jnp.arange(SLOTS, dtype=jnp.int32)[None, :]
    mover_x = movers[:, 0:1]
    mover_y = movers[:, 1:2]
    owner_x = along_x[gy_ids, gx_ids] * N_GY + gy_ids
    owner_y = gx_ids * N_GY + along_y[gx_ids, gy_ids]
    kept_rank = 2 + slot_ids - (slot_ids > mover_x).astype(jnp.int32) - (slot_ids > mover_y).astype(jnp.int32)
    kept_rank = jnp.clip(kept_rank, 0, SLOTS - 1)
    owners = jnp.where(slot_ids == mover_x, owner_x[:, None], jnp.where(slot_ids == mover_y, owner_y[:, None], device_ids[:, None]))
    items = jnp.where(slot_ids == mover_x, 0, jnp.where(slot_ids == mover_y, 1, kept_rank))
    slots_after = arrival[owners, items]
    return (owners.reshape(-1).astype(jnp.int32), slots_after.reshape(-1).astype(jnp.int32))


def draw_new_owner(key, part):
    tables = regrid_tables(key)
    return tables[0]


def draw_new_slot(key, part):
    tables = regrid_tables(key)
    return tables[1]


def draw_neighbours(key, part):
    key = jax.random.fold_in(key, 3)
    device_count = N_GX * N_GY
    layers = random_order(key, device_count, SLOTS)
    inverse = jnp.argsort(layers, axis=1).astype(jnp.int32)
    device_ids = jnp.arange(device_count, dtype=jnp.int32)
    gx_ids = device_ids // N_GY
    gy_ids = device_ids % N_GY

    def slot_at(gx_new, gy_new):
        return inverse[(gx_new * N_GY + gy_new)[:, None], layers]
    below_x = slot_at((gx_ids - 1) % N_GX, gy_ids)
    above_x = slot_at((gx_ids + 1) % N_GX, gy_ids)
    below_y = slot_at(gx_ids, (gy_ids - 1) % N_GY)
    above_y = slot_at(gx_ids, (gy_ids + 1) % N_GY)
    lower_layer = jnp.clip(layers - 1, 0, SLOTS - 1)
    upper_layer = jnp.clip(layers + 1, 0, SLOTS - 1)
    below_z = jnp.where(layers > 0, inverse[device_ids[:, None], lower_layer], -1)
    above_z = jnp.where(layers < SLOTS - 1, inverse[device_ids[:, None], upper_layer], -1)
    stacked = jnp.stack((below_x, above_x, below_y, above_y, below_z, above_z), axis=2)
    return stacked.reshape(device_count * SLOTS, 6).astype(jnp.int32)


def draw_old_state(key, part):
    key = jax.random.fold_in(key, 5)
    split_random_keys = jax.random.split(key, 3)
    total_boxes = N_GX * N_GY * SLOTS
    species_fractions = jax.random.uniform(split_random_keys[0], (total_boxes, NSPEC, BOX_CELL_TOTAL), jnp.float32)
    flow_velocity = jnp.clip(jax.random.normal(split_random_keys[1], (total_boxes, 3, BOX_CELL_TOTAL), jnp.float32), -4.0, 4.0)
    thermal_field = jax.random.uniform(split_random_keys[2], (total_boxes, 1, BOX_CELL_TOTAL), jnp.float32, 1.0, 3.0)
    return jnp.concatenate([species_fractions, flow_velocity, thermal_field], axis=1).astype(jnp.float32)


def setup_inputs(seed: int = 0) -> dict:
    arg_keys = jax.random.split(jax.random.key(seed), 10)
    old_state = draw_old_state(jax.random.fold_in(arg_keys[9], 71), 0)
    new_owner = draw_new_owner(jax.random.fold_in(arg_keys[9], 71), 0)
    new_slot = draw_new_slot(jax.random.fold_in(arg_keys[9], 71), 0)
    neighbours = draw_neighbours(jax.random.fold_in(arg_keys[9], 71), 0)
    diffusivity = jnp.clip(jnp.exp(jax.random.uniform(arg_keys[4], (COMPS,), jnp.float32, math.log(0.01), math.log(0.06))), 0.01, 0.06)
    stoichiometry = jnp.clip(jax.random.uniform(arg_keys[5], (NSPEC,), jnp.float32, -1.0, 1.0), -1.0, 1.0)
    heat_release = jnp.clip(jnp.exp(jax.random.uniform(arg_keys[6], (1,), jnp.float32, math.log(0.5), math.log(2.0))), 0.5, 2.0)
    prefactor = jnp.clip(jnp.exp(jax.random.uniform(arg_keys[7], (1,), jnp.float32, math.log(0.02), math.log(0.1))), 0.02, 0.1)
    activation = jnp.clip(jax.random.uniform(arg_keys[8], (1,), jnp.float32, 1.0, 3.0), 1.0, 3.0)
    return dict(old_state=old_state, new_owner=new_owner, new_slot=new_slot, neighbours=neighbours, diffusivity=diffusivity, stoichiometry=stoichiometry, heat_release=heat_release, prefactor=prefactor, activation=activation)


def side_slice(padded, axis_id, start_shift):
    index = [slice(None), slice(1, -1), slice(1, -1), slice(1, -1)]
    extent = padded.shape[axis_id]
    index[axis_id] = slice(1 + start_shift, extent - 1 + start_shift)
    return padded[tuple(index)]


def advance_box(one_box, ghost_xm, ghost_xp, ghost_ym, ghost_yp, ghost_zm, ghost_zp, diffusivity, source, prefactor, activation):
    padded = jnp.zeros((COMPS, BZ + 2, BX + 2, BX + 2), one_box.dtype)
    padded = padded.at[:, 1:-1, 1:-1, 1:-1].set(one_box)
    padded = padded.at[:, 1:-1, 1:-1, 0].set(ghost_xm)
    padded = padded.at[:, 1:-1, 1:-1, -1].set(ghost_xp)
    padded = padded.at[:, 1:-1, 0, 1:-1].set(ghost_ym)
    padded = padded.at[:, 1:-1, -1, 1:-1].set(ghost_yp)
    padded = padded.at[:, 0, 1:-1, 1:-1].set(ghost_zm)
    padded = padded.at[:, -1, 1:-1, 1:-1].set(ghost_zp)
    coefficient = diffusivity[:, None, None, None] * (padded[NSPEC + 3] ** 0.7)[None]
    center = padded[:, 1:-1, 1:-1, 1:-1]
    center_coef = coefficient[:, 1:-1, 1:-1, 1:-1]
    change = jnp.zeros_like(center)
    for axis_id in (1, 2, 3):
        for start_shift in (-1, 1):
            change = change + 0.5 * (center_coef + side_slice(coefficient, axis_id, start_shift)) * (side_slice(padded, axis_id, start_shift) - center)
    reaction_rate = prefactor[0] * center[0] * center[1] * jnp.exp(-activation[0] / center[NSPEC + 3])
    return center + change + source[:, None, None, None] * reaction_rate[None]


def reference(old_state, new_owner, new_slot, neighbours, diffusivity, stoichiometry, heat_release, prefactor, activation):
    total_boxes = old_state.shape[0]
    target = (new_owner * SLOTS + new_slot).astype(jnp.int32)
    regridded = jnp.zeros_like(old_state).at[target].set(old_state)
    regridded = regridded.reshape(total_boxes, COMPS, BZ, BX, BX)
    box_ids = jnp.arange(total_boxes, dtype=jnp.int32)
    owner_ids = box_ids // SLOTS
    gx_ids = owner_ids // N_GY
    gy_ids = owner_ids % N_GY
    below_x = (((gx_ids - 1) % N_GX) * N_GY + gy_ids) * SLOTS + neighbours[:, 0]
    above_x = (((gx_ids + 1) % N_GX) * N_GY + gy_ids) * SLOTS + neighbours[:, 1]
    below_y = (gx_ids * N_GY + (gy_ids - 1) % N_GY) * SLOTS + neighbours[:, 2]
    above_y = (gx_ids * N_GY + (gy_ids + 1) % N_GY) * SLOTS + neighbours[:, 3]
    below_z = owner_ids * SLOTS + jnp.maximum(neighbours[:, 4], 0)
    above_z = owner_ids * SLOTS + jnp.maximum(neighbours[:, 5], 0)
    edge_low = (neighbours[:, 4] < 0)[:, None, None, None]
    edge_high = (neighbours[:, 5] < 0)[:, None, None, None]
    source = jnp.concatenate([stoichiometry, jnp.zeros((3,), jnp.float32), heat_release])

    def one_step(entries):
        return advance_box(*entries, diffusivity, source, prefactor, activation)

    for step_index in range(STEPS):
        ghost_xm = regridded[below_x, :, :, :, BX - 1]
        ghost_xp = regridded[above_x, :, :, :, 0]
        ghost_ym = regridded[below_y, :, :, BX - 1, :]
        ghost_yp = regridded[above_y, :, :, 0, :]
        ghost_zm = jnp.where(edge_low, regridded[:, :, 0], regridded[below_z, :, BZ - 1])
        ghost_zp = jnp.where(edge_high, regridded[:, :, BZ - 1], regridded[above_z, :, 0])
        regridded = lax.map(one_step, (regridded, ghost_xm, ghost_xp, ghost_ym, ghost_yp, ghost_zm, ghost_zp))
    return regridded.reshape(total_boxes, COMPS, BOX_CELL_TOTAL)
```

```python
import functools

import jax
import jax.numpy as jnp
from jax import lax
from jax.experimental import pallas as pl
from jax.experimental.pallas import tpu as pltpu
from jax.sharding import PartitionSpec as P

NSPEC = 9
COMPS = 13
TEMP = 12
BX = 32
BZ = 16
SLOTS = 2
STEPS = 3
LAYERS = SLOTS * BZ
LROWS = COMPS * 8
BROWS = BZ * LROWS
ROWS = SLOTS * BROWS
TAG = 8
PIECE = LROWS + TAG
YBOX = BROWS + TAG
NONE = -1.0
SMEM = pltpu.SMEM
VMEM = pltpu.VMEM
F32 = jnp.float32
PARAMS = pltpu.CompilerParams(vmem_limit_bytes=48 * 1024 * 1024)


def shifted(value, axis, steps):
    count = lax.axis_size(axis)
    pairs = [(source, (source + steps) % count) for source in range(count)]
    return lax.ppermute(value, axis, pairs)


def moves(owner_ref, row, count_y, index_x, index_y):
    owner = owner_ref[row]
    dest_x = owner // count_y
    dest_y = owner - dest_x * count_y
    goes_x = (dest_y == index_y) & (dest_x != index_x)
    goes_y = (dest_x == index_x) & (dest_y != index_y)
    return dest_x, dest_y, goes_x, goes_y


def pack_kernel(count_y, owner_ref, slot_ref, old_ref, box_ref, outx_ref, outy_ref):
    index_x = lax.axis_index("gx")
    index_y = lax.axis_index("gy")

    def layer(z, carry):
        for n in range(SLOTS):
            row = pl.multiple_of(n * BROWS + z * LROWS, 8)
            for t in range(8):
                cells = pl.ds(pl.multiple_of(z * 1024 + t * 128, 128), 128)
                box_ref[pl.ds(row + t, COMPS, stride=8), :] = old_ref[n, :, cells]
        return carry

    lax.fori_loop(0, BZ, layer, 0)
    row_x = jnp.int32(0)
    row_y = jnp.int32(0)
    tag_x = jnp.int32(-1)
    tag_y = jnp.int32(-1)
    for n in range(SLOTS):
        dest_x, dest_y, goes_x, goes_y = moves(owner_ref, n, count_y, index_x, index_y)
        row_x = jnp.where(goes_x, n, row_x)
        row_y = jnp.where(goes_y, n, row_y)
        tag_x = jnp.where(goes_x, dest_x * SLOTS + slot_ref[n], tag_x)
        tag_y = jnp.where(goes_y, dest_y * SLOTS + slot_ref[n], tag_y)

    def copy(z, carry):
        source_x = pl.ds(pl.multiple_of(row_x * BROWS + z * LROWS, 8), LROWS)
        source_y = pl.ds(pl.multiple_of(row_y * BROWS + z * LROWS, 8), LROWS)
        outx_ref[z, :LROWS, :] = box_ref[source_x, :]
        outx_ref[z, LROWS:, :] = jnp.full((TAG, 128), tag_x, jnp.int32).astype(F32)
        outy_ref[0, pl.ds(pl.multiple_of(z * LROWS, 8), LROWS), :] = box_ref[source_y, :]
        return carry

    lax.fori_loop(0, BZ, copy, 0)
    outy_ref[0, BROWS:, :] = jnp.full((TAG, 128), tag_y, jnp.int32).astype(F32)


def tag_of(tile):
    return jnp.max(tile).astype(jnp.int32)


def sort_kernel(pieces_ref, first_ref, second_ref, more_ref, used_ref):
    count = pieces_ref.shape[0]
    empty = jnp.full((TAG, 128), NONE, F32)
    more_ref[0] = 0
    tags = []
    for d in range(count):
        first_ref[d, LROWS:, :] = empty
        second_ref[d, LROWS:, :] = empty
        used_ref[d] = 0
        tags.append(tag_of(pieces_ref[d, LROWS:, :]))
    for s in range(count):
        tag = tags[s]
        there = jnp.maximum(tag, 0) // SLOTS
        used = used_ref[there]

        @pl.when((tag >= 0) & (used == 0))
        def _():
            first_ref[there, :, :] = pieces_ref[s]
            used_ref[there] = 1

        @pl.when((tag >= 0) & (used == 1))
        def _():
            second_ref[there, :, :] = pieces_ref[s]
            more_ref[0] = 1


def roll(value, shift, axis):
    if isinstance(shift, int):
        shift = shift % value.shape[axis]
        if shift == 0:
            return value
        return pltpu.roll(value, shift, axis)
    return pltpu.roll(value, lax.rem(shift + 256, 128), axis)


def lanes():
    return lax.broadcasted_iota(jnp.int32, (8, 128), 1)


def sublanes():
    return lax.broadcasted_iota(jnp.int32, (8, 128), 0)


def put_x_faces(layer_index, c, value, low_ref, high_ref):
    here = (lanes() & 31) == layer_index
    rows = pl.ds(c * 8, 8)
    low_ref[rows, :] = jnp.where(here, roll(value, layer_index, 1), low_ref[rows, :])
    high_ref[rows, :] = jnp.where(here, roll(value, layer_index - 31, 1), high_ref[rows, :])


def put_y_faces(state_ref, low_ref, high_ref):
    group = lanes() >> 5

    for c in range(COMPS):
        low = jnp.zeros((8, 128), F32)
        high = jnp.zeros((8, 128), F32)
        for n in range(SLOTS):
            for half in range(2):
                where = 2 * n + half
                base = n * BROWS + half * 8 * LROWS + c * 8
                bottom = state_ref[pl.ds(base, 8, stride=LROWS), :]
                top = state_ref[pl.ds(base + 7, 8, stride=LROWS), :]
                low = jnp.where(group == where, roll(bottom, 32 * where, 1), low)
                high = jnp.where(group == where, roll(top, 32 * where - 96, 1), high)
        low_ref[c * 8 : c * 8 + 8, :] = low
        high_ref[c * 8 : c * 8 + 8, :] = high


def place_kernel(
    count_y, owner_ref, slot_ref, box_ref, first_ref, second_ref, ally_ref,
    state_ref, xl_ref, xh_ref, yl_ref, yh_ref, tagx_ref, tagy_ref, tag_sem, sems,
):
    index_x = lax.axis_index("gx")
    index_y = lax.axis_index("gy")
    loads = [
        pltpu.make_async_copy(ally_ref.at[:, pl.ds(BROWS, TAG), :], tagy_ref, tag_sem.at[0]),
        pltpu.make_async_copy(first_ref.at[0, pl.ds(LROWS, TAG), :], tagx_ref.at[0], tag_sem.at[1]),
        pltpu.make_async_copy(second_ref.at[0, pl.ds(LROWS, TAG), :], tagx_ref.at[1], tag_sem.at[2]),
    ]
    for load in loads:
        load.start()
    for load in loads:
        load.wait()

    def into(slot):
        return state_ref.at[pl.ds(slot * BROWS, BROWS), :]

    for n in range(SLOTS):
        dest_x, dest_y, goes_x, goes_y = moves(owner_ref, n, count_y, index_x, index_y)
        slot = slot_ref[n]

        @pl.when((dest_x == index_x) & (dest_y == index_y))
        def _():
            pltpu.make_async_copy(box_ref.at[pl.ds(n * BROWS, BROWS), :], into(slot), sems.at[slot]).start()

    for k, source in enumerate((first_ref, second_ref)):
        tag = tag_of(tagx_ref[k])

        @pl.when(tag >= 0)
        def _():
            slot = lax.rem(tag, SLOTS)
            for z in range(BZ):
                rows = pl.ds(pl.multiple_of(slot * BROWS + z * LROWS, 8), LROWS)
                pltpu.make_async_copy(
                    source.at[z, pl.ds(0, LROWS), :], state_ref.at[rows, :], sems.at[slot]
                ).start()

    for p in range(tagy_ref.shape[0]):
        tag = tag_of(tagy_ref[p])

        @pl.when((tag >= 0) & (tag // SLOTS == index_y))
        def _():
            slot = lax.rem(tag, SLOTS)
            pltpu.make_async_copy(ally_ref.at[p, pl.ds(0, BROWS), :], into(slot), sems.at[slot]).start()

    for slot in range(SLOTS):
        pltpu.make_async_copy(box_ref.at[pl.ds(0, BROWS), :], into(slot), sems.at[slot]).wait()

    def layer(index, carry):
        row = pl.multiple_of(index * LROWS, 8)
        for c in range(COMPS):
            put_x_faces(index, c, state_ref[pl.ds(row + c * 8, 8), :], xl_ref, xh_ref)
        return carry

    xl_ref[...] = jnp.zeros_like(xl_ref)
    xh_ref[...] = jnp.zeros_like(xh_ref)
    lax.fori_loop(0, LAYERS, layer, 0)
    put_y_faces(state_ref, yl_ref, yh_ref)


def power(value):
    return jnp.exp(0.7 * jnp.log(value))


def step_kernel(
    last, near_ref, diff_ref, stoi_ref, heat_ref, pre_ref, act_ref,
    state_ref, bx_ref, ax_ref, by_ref, ay_ref, *rest,
):
    if last:
        out_ref, coef_ref, gx_ref, ym_ref, yp_ref, new_ref = rest
    else:
        new_ref, xl_ref, xh_ref, yl_ref, yh_ref, coef_ref, gx_ref, ym_ref, yp_ref = rest
    lane = lanes()
    sub = sublanes()
    x_first = (lane & 31) == 0
    x_last = (lane & 31) == 31
    y_low_lanes = lane < 32
    y_high_lanes = lane >= 96
    sub_first = sub == 0
    sub_last = sub == 7

    def power_layer(index, carry):
        row = pl.multiple_of(index * LROWS, 8)
        coef_ref[pl.ds(pl.multiple_of(index * 8, 8), 8), :] = power(state_ref[pl.ds(row + TEMP * 8, 8), :])
        return carry

    lax.fori_loop(0, LAYERS, power_layer, 0)
    gx_ref[0] = power(bx_ref[TEMP * 8 :, :])
    gx_ref[1] = power(ax_ref[TEMP * 8 :, :])
    for c in range(COMPS + 1):
        if c < COMPS:
            below = by_ref[c * 8 : c * 8 + 8, :]
            above = ay_ref[c * 8 : c * 8 + 8, :]
        else:
            below = power(by_ref[TEMP * 8 :, :])
            above = power(ay_ref[TEMP * 8 :, :])
        for n in range(SLOTS):
            from_below = near_ref[n, 2]
            from_above = near_ref[n, 3]
            for half in range(2):
                rows = pl.ds((n * (COMPS + 1) + c) * BZ + half * 8, 8)
                ym_ref[rows, :] = roll(below, -32 * (2 * from_below + half), 1)
                yp_ref[rows, :] = roll(above, 96 - 32 * (2 * from_above + half), 1)
    if not last:
        xl_ref[...] = jnp.zeros_like(xl_ref)
        xh_ref[...] = jnp.zeros_like(xh_ref)

    def layer(index, carry):
        n = index // BZ
        z = index - n * BZ
        near_zm = near_ref[n, 4]
        near_zp = near_ref[n, 5]
        index_m = jnp.where(z == 0, jnp.where(near_zm < 0, index, near_zm * BZ + BZ - 1), index - 1)
        index_p = jnp.where(z == BZ - 1, jnp.where(near_zp < 0, index, near_zp * BZ), index + 1)
        shift_m = 128 - (near_ref[n, 0] * BZ + z)
        shift_p = 128 + 31 - (near_ref[n, 1] * BZ + z)

        def beside(value, face_m, face_p, y_row):
            xm = jnp.where(x_first, roll(face_m, shift_m, 1), roll(value, 1, 1))
            xp = jnp.where(x_last, roll(face_p, shift_p, 1), roll(value, -1, 1))
            down = roll(value, 32, 1)
            ghost = jnp.broadcast_to(ym_ref[pl.ds(y_row, 1), :], (8, 128))
            ym = jnp.where(y_low_lanes, jnp.where(sub_first, ghost, roll(down, 1, 0)), down)
            up = roll(value, -32, 1)
            ghost = jnp.broadcast_to(yp_ref[pl.ds(y_row, 1), :], (8, 128))
            yp = jnp.where(y_high_lanes, jnp.where(sub_last, ghost, roll(up, -1, 0)), up)
            return xm, xp, ym, yp

        def coef(at):
            return coef_ref[pl.ds(pl.multiple_of(at * 8, 8), 8), :]

        y_row = n * (COMPS + 1) * BZ + z
        center = coef(index)
        sides = beside(center, gx_ref[0], gx_ref[1], y_row + COMPS * BZ)
        weights = [0.5 * (center + side) for side in sides + (coef(index_m), coef(index_p))]
        total = functools.reduce(lambda a, b: a + b, weights)
        row = pl.multiple_of(index * LROWS, 8)
        row_m = pl.multiple_of(index_m * LROWS, 8)
        row_p = pl.multiple_of(index_p * LROWS, 8)
        rate = (
            pre_ref[0]
            * state_ref[pl.ds(row, 8), :]
            * state_ref[pl.ds(row + 8, 8), :]
            * jnp.exp(-act_ref[0] / state_ref[pl.ds(row + TEMP * 8, 8), :])
        )
        for c in range(COMPS):
            rows = slice(c * 8, c * 8 + 8)
            value = state_ref[pl.ds(row + c * 8, 8), :]
            sides = beside(value, bx_ref[rows, :], ax_ref[rows, :], y_row + c * BZ)
            sides = sides + (state_ref[pl.ds(row_m + c * 8, 8), :], state_ref[pl.ds(row_p + c * 8, 8), :])
            change = -total * value
            for weight, side in zip(weights, sides):
                change = change + weight * side
            value = value + diff_ref[c] * change
            if c < NSPEC:
                value = value + stoi_ref[c] * rate
            elif c == TEMP:
                value = value + heat_ref[0] * rate
            new_ref[pl.ds(row + c * 8, 8), :] = value
            if not last:
                put_x_faces(index, c, value, xl_ref, xh_ref)
        if last:
            for t in range(8):
                cells = pl.ds(pl.multiple_of(z * 1024 + t * 128, 128), 128)
                out_ref[n, :, cells] = new_ref[pl.ds(row + t, COMPS, stride=8), :]
        return carry

    lax.fori_loop(0, LAYERS, layer, 0)
    if not last:
        put_y_faces(new_ref, yl_ref, yh_ref)


def spec(space):
    return pl.BlockSpec(memory_space=space)


def struct(*shape, dtype=F32):
    return jax.ShapeDtypeStruct(shape, dtype)


PLANES = [struct(LROWS, 128)] * 4


def step(last, near, constants, state, planes):
    scratch = [
        VMEM((LAYERS * 8, 128), F32),
        VMEM((2, 8, 128), F32),
        VMEM((SLOTS * (COMPS + 1) * BZ, 128), F32),
        VMEM((SLOTS * (COMPS + 1) * BZ, 128), F32),
    ]
    if last:
        out_shape = struct(SLOTS, COMPS, BZ * BX * BX)
        out_specs = spec(VMEM)
        scratch.append(VMEM((ROWS, 128), F32))
    else:
        out_shape = [struct(ROWS, 128)] + PLANES
        out_specs = [spec(VMEM)] * 5
    return pl.pallas_call(
        functools.partial(step_kernel, last),
        out_shape=out_shape,
        in_specs=[spec(SMEM)] * 6 + [spec(VMEM)] * 5,
        out_specs=out_specs,
        scratch_shapes=scratch,
        compiler_params=PARAMS,
        cost_estimate=pl.CostEstimate(flops=20_000_000, bytes_accessed=4_000_000, transcendentals=0),
        name="step_last" if last else "step",
    )(near, *constants, state, *planes)


def shards(
    old_state,
    new_owner,
    new_slot,
    neighbours,
    diffusivity,
    stoichiometry,
    heat_release,
    prefactor,
    activation,
):
    count_x = lax.axis_size("gx")
    count_y = lax.axis_size("gy")
    boxes, outbox_x, outbox_y = pl.pallas_call(
        functools.partial(pack_kernel, count_y),
        out_shape=[struct(ROWS, 128), struct(BZ, PIECE, 128), struct(1, YBOX, 128)],
        in_specs=[spec(SMEM)] * 2 + [spec(VMEM)],
        out_specs=[spec(VMEM)] * 3,
        compiler_params=PARAMS,
        name="pack",
    )(new_owner, new_slot, old_state)
    all_y = lax.all_gather(outbox_y, "gy", axis=0, tiled=True)
    pieces = lax.all_to_all(outbox_x, "gx", 0, 0, tiled=True)
    first, second, more = pl.pallas_call(
        sort_kernel,
        out_shape=[struct(count_x, PIECE, 128)] * 2 + [struct(1, dtype=jnp.int32)],
        in_specs=[spec(VMEM)],
        out_specs=[spec(VMEM)] * 2 + [spec(SMEM)],
        scratch_shapes=[SMEM((count_x,), jnp.int32)],
        compiler_params=PARAMS,
        name="sort",
    )(pieces)
    first = lax.all_to_all(first, "gx", 0, 0, tiled=True)
    second = lax.cond(
        more[0] > 0,
        lambda value: lax.all_to_all(value, "gx", 0, 0, tiled=True),
        lambda value: value,
        second,
    )
    state, *planes = pl.pallas_call(
        functools.partial(place_kernel, count_y),
        out_shape=[struct(ROWS, 128)] + PLANES,
        in_specs=[spec(SMEM)] * 2 + [spec(pl.ANY)] * 4,
        out_specs=[spec(VMEM)] * 5,
        scratch_shapes=[
            VMEM((2, TAG, 128), F32),
            VMEM((count_y, TAG, 128), F32),
            pltpu.SemaphoreType.DMA((3,)),
            pltpu.SemaphoreType.DMA((SLOTS,)),
        ],
        compiler_params=PARAMS,
        name="place",
    )(new_owner, new_slot, boxes, first, second, all_y)
    constants = (diffusivity, stoichiometry, heat_release, prefactor, activation)
    for step_index in range(STEPS):
        x_low, x_high, y_low, y_high = planes
        received = (
            shifted(x_high, "gx", 1),
            shifted(x_low, "gx", -1),
            shifted(y_high, "gy", 1),
            shifted(y_low, "gy", -1),
        )
        if step_index < STEPS - 1:
            state, *planes = step(False, neighbours, constants, state, received)
        else:
            state = step(True, neighbours, constants, state, received)
    return state


def solution(mesh):
    return jax.shard_map(
        shards,
        mesh=mesh,
        in_specs=(
            P(("gx", "gy"), None, None),
            P(("gx", "gy")),
            P(("gx", "gy")),
            P(("gx", "gy"), None),
            P(),
            P(),
            P(),
            P(),
            P(),
        ),
        out_specs=P(("gx", "gy"), None, None),
        check_vma=False,
    )
```

```python
import functools

import jax
import jax.numpy as jnp
from jax import lax
from jax.experimental import pallas as pl
from jax.experimental.pallas import tpu as pltpu
from jax.sharding import PartitionSpec as P

NSPEC = 9
COMPS = 13
TEMP = 12
BX = 32
BZ = 16
SLOTS = 2
STEPS = 3
LAYERS = SLOTS * BZ
LROWS = COMPS * 8
BROWS = BZ * LROWS
ROWS = SLOTS * BROWS
TAG = 8
PIECE = LROWS + TAG
YBOX = BROWS + TAG
NONE = -1.0
SMEM = pltpu.SMEM
VMEM = pltpu.VMEM
F32 = jnp.float32
PARAMS = pltpu.CompilerParams(vmem_limit_bytes=48 * 1024 * 1024)


def swapped(value, axis, first):
    count = lax.axis_size(axis)
    pairs = []
    for low in range(first, count + first, 2):
        pairs += [(low % count, (low + 1) % count), ((low + 1) % count, low % count)]
    return lax.ppermute(value, axis, pairs)


def moves(owner_ref, row, count_y, index_x, index_y):
    owner = owner_ref[row]
    dest_x = owner // count_y
    dest_y = owner - dest_x * count_y
    goes_x = (dest_y == index_y) & (dest_x != index_x)
    goes_y = (dest_x == index_x) & (dest_y != index_y)
    return dest_x, dest_y, goes_x, goes_y


def source_rows(n, z, c):
    return pl.ds(c * 256 + z * 16 + n, 8, stride=2)


def pack_kernel(count_y, owner_ref, slot_ref, old_ref, box_ref, outx_ref, outy_ref):
    index_x = lax.axis_index("gx")
    index_y = lax.axis_index("gy")
    row_x = jnp.int32(0)
    row_y = jnp.int32(0)
    tag_x = jnp.int32(-1)
    tag_y = jnp.int32(-1)
    for n in range(SLOTS):
        dest_x, dest_y, goes_x, goes_y = moves(owner_ref, n, count_y, index_x, index_y)
        row_x = jnp.where(goes_x, n, row_x)
        row_y = jnp.where(goes_y, n, row_y)
        tag_x = jnp.where(goes_x, dest_x * SLOTS + slot_ref[n], tag_x)
        tag_y = jnp.where(goes_y, dest_y * SLOTS + slot_ref[n], tag_y)

    def layer(z, carry):
        row = pl.multiple_of(z * LROWS, 8)
        for c in range(COMPS):
            for n in range(SLOTS):
                box_ref[pl.ds(n * BROWS + row + c * 8, 8), :] = old_ref[source_rows(n, z, c), :]
            outx_ref[z, c * 8 : c * 8 + 8, :] = old_ref[source_rows(row_x, z, c), :]
            outy_ref[0, pl.ds(row + c * 8, 8), :] = old_ref[source_rows(row_y, z, c), :]
        outx_ref[z, LROWS:, :] = jnp.full((TAG, 128), tag_x, jnp.int32).astype(F32)
        return carry

    lax.fori_loop(0, BZ, layer, 0)
    outy_ref[0, BROWS:, :] = jnp.full((TAG, 128), tag_y, jnp.int32).astype(F32)


def tag_of(tile):
    return jnp.max(tile).astype(jnp.int32)


def sort_kernel(pieces_ref, first_ref, second_ref, more_ref, used_ref):
    count = pieces_ref.shape[0]
    empty = jnp.full((TAG, 128), NONE, F32)
    more_ref[0] = 0
    tags = []
    for d in range(count):
        first_ref[d, LROWS:, :] = empty
        second_ref[d, LROWS:, :] = empty
        used_ref[d] = 0
        tags.append(tag_of(pieces_ref[d, LROWS:, :]))
    for s in range(count):
        tag = tags[s]
        there = jnp.maximum(tag, 0) // SLOTS
        used = used_ref[there]

        @pl.when((tag >= 0) & (used == 0))
        def _():
            first_ref[there, :, :] = pieces_ref[s]
            used_ref[there] = 1

        @pl.when((tag >= 0) & (used == 1))
        def _():
            second_ref[there, :, :] = pieces_ref[s]
            more_ref[0] = 1


def roll(value, shift, axis):
    if isinstance(shift, int):
        shift = shift % value.shape[axis]
        if shift == 0:
            return value
        return pltpu.roll(value, shift, axis)
    return pltpu.roll(value, lax.rem(shift + 256, 128), axis)


def lanes():
    return lax.broadcasted_iota(jnp.int32, (8, 128), 1)


def sublanes():
    return lax.broadcasted_iota(jnp.int32, (8, 128), 0)


def tile(row):
    return pl.ds(pl.multiple_of(row, 8), 8)


def put_faces(state_ref, out_refs):
    lane = lanes()
    ends = ((lane & 31) == 0) | ((lane & 31) == 31)
    even = (lane & 1) == 0
    group = lane >> 5
    even_x = lax.rem(lax.axis_index("gx"), 2) == 0
    even_y = lax.rem(lax.axis_index("gy"), 2) == 0
    xa_ref, xb_ref, ya_ref, yb_ref = out_refs

    def plane(c, carry):
        first = pl.multiple_of(c * 8, 8)
        rows = pl.ds(first, 8)
        both = []
        for n in range(SLOTS):
            parts = [
                roll(jnp.where(ends, state_ref[tile(first + (n * BZ + z) * LROWS), :], 0.0), 2 * z, 1)
                for z in range(BZ)
            ]
            while len(parts) > 1:
                parts = [a + b for a, b in zip(parts[::2], parts[1::2])]
            both.append(parts[0])
        other = roll(both[1], 1, 1)
        low = jnp.where(even, both[0], other)
        high = jnp.where(even, other, both[0])
        xa_ref[rows, :] = jnp.where(even_x, high, low)
        xb_ref[rows, :] = jnp.where(even_x, low, high)
        low = jnp.zeros((8, 128), F32)
        high = jnp.zeros((8, 128), F32)
        for n in range(SLOTS):
            for half in range(2):
                where = 2 * n + half
                base = n * BROWS + half * 8 * LROWS + first
                bottom = state_ref[pl.ds(base, 8, stride=LROWS), :]
                top = state_ref[pl.ds(base + 7, 8, stride=LROWS), :]
                low = jnp.where(group == where, roll(bottom, 32 * where, 1), low)
                high = jnp.where(group == where, roll(top, 32 * where - 96, 1), high)
        ya_ref[rows, :] = jnp.where(even_y, high, low)
        yb_ref[rows, :] = jnp.where(even_y, low, high)
        return carry

    lax.fori_loop(0, COMPS, plane, 0)


def place_kernel(
    count_y, owner_ref, slot_ref, box_ref, first_ref, second_ref, ally_ref,
    state_ref, xa_ref, xb_ref, ya_ref, yb_ref, tagx_ref, tagy_ref, tag_sem, sems,
):
    index_x = lax.axis_index("gx")
    index_y = lax.axis_index("gy")
    loads = [
        pltpu.make_async_copy(ally_ref.at[:, pl.ds(BROWS, TAG), :], tagy_ref, tag_sem.at[0]),
        pltpu.make_async_copy(first_ref.at[0, pl.ds(LROWS, TAG), :], tagx_ref.at[0], tag_sem.at[1]),
        pltpu.make_async_copy(second_ref.at[0, pl.ds(LROWS, TAG), :], tagx_ref.at[1], tag_sem.at[2]),
    ]
    for load in loads:
        load.start()
    for load in loads:
        load.wait()

    def into(slot):
        return state_ref.at[pl.ds(slot * BROWS, BROWS), :]

    for n in range(SLOTS):
        dest_x, dest_y, goes_x, goes_y = moves(owner_ref, n, count_y, index_x, index_y)
        slot = slot_ref[n]

        @pl.when((dest_x == index_x) & (dest_y == index_y))
        def _():
            pltpu.make_async_copy(box_ref.at[pl.ds(n * BROWS, BROWS), :], into(slot), sems.at[slot]).start()

    for k, source in enumerate((first_ref, second_ref)):
        tag = tag_of(tagx_ref[k])

        @pl.when(tag >= 0)
        def _():
            slot = lax.rem(tag, SLOTS)
            for z in range(BZ):
                rows = pl.ds(pl.multiple_of(slot * BROWS + z * LROWS, 8), LROWS)
                pltpu.make_async_copy(
                    source.at[z, pl.ds(0, LROWS), :], state_ref.at[rows, :], sems.at[slot]
                ).start()

    for p in range(tagy_ref.shape[0]):
        tag = tag_of(tagy_ref[p])

        @pl.when((tag >= 0) & (tag // SLOTS == index_y))
        def _():
            slot = lax.rem(tag, SLOTS)
            pltpu.make_async_copy(ally_ref.at[p, pl.ds(0, BROWS), :], into(slot), sems.at[slot]).start()

    for slot in range(SLOTS):
        pltpu.make_async_copy(box_ref.at[pl.ds(0, BROWS), :], into(slot), sems.at[slot]).wait()

    put_faces(state_ref, (xa_ref, xb_ref, ya_ref, yb_ref))


def power(value):
    return jnp.exp(0.7 * jnp.log(value))


UNROLL = 4


def step_kernel(
    last, near_ref, diff_ref, stoi_ref, heat_ref, pre_ref, act_ref,
    state_ref, xa_ref, xb_ref, ya_ref, yb_ref, *rest,
):
    if last:
        new_ref, coef_ref, gx_ref, ym_ref, yp_ref = rest
    else:
        new_ref, *out_refs, coef_ref, gx_ref, ym_ref, yp_ref = rest
    lane = lanes()
    sub = sublanes()
    even = (lane & 1) == 0
    x_first = (lane & 31) == 0
    x_last = (lane & 31) == 31
    y_low_lanes = lane < 32
    y_high_lanes = lane >= 96
    sub_first = sub == 0
    sub_last = sub == 7
    even_x = lax.rem(lax.axis_index("gx"), 2) == 0
    even_y = lax.rem(lax.axis_index("gy"), 2) == 0

    def power_layer(block, carry):
        for u in range(8):
            index = block * 8 + u
            coef_ref[tile(index * 8), :] = power(state_ref[tile(index * LROWS + TEMP * 8), :])
        return carry

    lax.fori_loop(0, LAYERS // 8, power_layer, 0)
    for c in range(COMPS):
        rows = slice(c * 8, c * 8 + 8)
        pair_a, pair_b = xa_ref[rows, :], xb_ref[rows, :]
        below = jnp.where(even_x, pair_b, pair_a)
        above = jnp.where(even_x, pair_a, pair_b)
        for n in range(SLOTS):
            ghost = jnp.where(
                even, roll(below, -31 - near_ref[n, 0], 1), roll(above, 31 - near_ref[n, 1], 1)
            )
            gx_ref[n * (COMPS + 1) + c] = ghost
            if c == TEMP:
                gx_ref[n * (COMPS + 1) + COMPS] = power(ghost)
        pair_a, pair_b = ya_ref[rows, :], yb_ref[rows, :]
        below = jnp.where(even_y, pair_b, pair_a)
        above = jnp.where(even_y, pair_a, pair_b)
        for n in range(SLOTS):
            for half in range(2):
                ghost_m = roll(below, -32 * (2 * near_ref[n, 2] + half), 1)
                ghost_p = roll(above, 96 - 32 * (2 * near_ref[n, 3] + half), 1)
                at = (n * (COMPS + 1) + c) * BZ + half * 8
                ym_ref[pl.ds(at, 8), :] = ghost_m
                yp_ref[pl.ds(at, 8), :] = ghost_p
                if c == TEMP:
                    ym_ref[pl.ds(at + BZ, 8), :] = power(ghost_m)
                    yp_ref[pl.ds(at + BZ, 8), :] = power(ghost_p)

    def layer(n, z):
        index = n * BZ + z
        near_zm = near_ref[n, 4]
        near_zp = near_ref[n, 5]
        index_m = jnp.where(z == 0, jnp.where(near_zm < 0, index, near_zm * BZ + BZ - 1), index - 1)
        index_p = jnp.where(z == BZ - 1, jnp.where(near_zp < 0, index, near_zp * BZ), index + 1)
        shift = 128 - 2 * z

        def beside(value, c):
            ghost = roll(gx_ref[n * (COMPS + 1) + c], shift, 1)
            xm = jnp.where(x_first, ghost, roll(value, 1, 1))
            xp = jnp.where(x_last, ghost, roll(value, -1, 1))
            y_row = (n * (COMPS + 1) + c) * BZ + z
            down = roll(value, 32, 1)
            ghost = jnp.broadcast_to(ym_ref[pl.ds(y_row, 1), :], (8, 128))
            ym = jnp.where(y_low_lanes, jnp.where(sub_first, ghost, roll(down, 1, 0)), down)
            up = roll(value, -32, 1)
            ghost = jnp.broadcast_to(yp_ref[pl.ds(y_row, 1), :], (8, 128))
            yp = jnp.where(y_high_lanes, jnp.where(sub_last, ghost, roll(up, -1, 0)), up)
            return xm, xp, ym, yp

        center = coef_ref[tile(index * 8), :]
        sides = beside(center, COMPS) + (coef_ref[tile(index_m * 8), :], coef_ref[tile(index_p * 8), :])
        weights = [0.5 * (center + side) for side in sides]
        total = functools.reduce(lambda a, b: a + b, weights)
        row = pl.multiple_of(index * LROWS, 8)
        row_m = pl.multiple_of(index_m * LROWS, 8)
        row_p = pl.multiple_of(index_p * LROWS, 8)
        rate = (
            pre_ref[0]
            * state_ref[pl.ds(row, 8), :]
            * state_ref[pl.ds(row + 8, 8), :]
            * jnp.exp(-act_ref[0] / state_ref[pl.ds(row + TEMP * 8, 8), :])
        )
        for c in range(COMPS):
            value = state_ref[pl.ds(row + c * 8, 8), :]
            sides = beside(value, c)
            sides = sides + (state_ref[pl.ds(row_m + c * 8, 8), :], state_ref[pl.ds(row_p + c * 8, 8), :])
            change = -total * value
            for weight, side in zip(weights, sides):
                change = change + weight * side
            value = value + diff_ref[c] * change
            if c < NSPEC:
                value = value + stoi_ref[c] * rate
            elif c == TEMP:
                value = value + heat_ref[0] * rate
            if last:
                new_ref[source_rows(n, z, c), :] = value
            else:
                new_ref[pl.ds(row + c * 8, 8), :] = value

    def layers(block, carry):
        n = block // (BZ // UNROLL)
        z = (block - n * (BZ // UNROLL)) * UNROLL
        for u in range(UNROLL):
            layer(n, z + u)
        return carry

    lax.fori_loop(0, LAYERS // UNROLL, layers, 0)
    if not last:
        put_faces(new_ref, out_refs)


def spec(space):
    return pl.BlockSpec(memory_space=space)


def struct(*shape, dtype=F32):
    return jax.ShapeDtypeStruct(shape, dtype)


PLANES = [struct(LROWS, 128)] * 4


def step(last, near, constants, state, planes):
    if last:
        out_shape = struct(ROWS, 128)
        out_specs = spec(VMEM)
    else:
        out_shape = [struct(ROWS, 128)] + PLANES
        out_specs = [spec(VMEM)] * 5
    return pl.pallas_call(
        functools.partial(step_kernel, last),
        out_shape=out_shape,
        in_specs=[spec(SMEM)] * 6 + [spec(VMEM)] * 5,
        out_specs=out_specs,
        scratch_shapes=[
            VMEM((LAYERS * 8, 128), F32),
            VMEM((SLOTS * (COMPS + 1), 8, 128), F32),
            VMEM((SLOTS * (COMPS + 1) * BZ, 128), F32),
            VMEM((SLOTS * (COMPS + 1) * BZ, 128), F32),
        ],
        compiler_params=PARAMS,
        cost_estimate=pl.CostEstimate(flops=20_000_000, bytes_accessed=4_000_000, transcendentals=0),
        name="step_last" if last else "step",
    )(near, *constants, state, *planes)


def shards(
    old_state,
    new_owner,
    new_slot,
    neighbours,
    diffusivity,
    stoichiometry,
    heat_release,
    prefactor,
    activation,
):
    count_x = lax.axis_size("gx")
    count_y = lax.axis_size("gy")
    old_rows = old_state.reshape(SLOTS, COMPS, 128, 128).transpose(1, 2, 0, 3).reshape(ROWS, 128)
    boxes, outbox_x, outbox_y = pl.pallas_call(
        functools.partial(pack_kernel, count_y),
        out_shape=[struct(ROWS, 128), struct(BZ, PIECE, 128), struct(1, YBOX, 128)],
        in_specs=[spec(SMEM)] * 2 + [spec(VMEM)],
        out_specs=[spec(VMEM)] * 3,
        compiler_params=PARAMS,
        name="pack",
    )(new_owner, new_slot, old_rows)
    all_y = lax.all_gather(outbox_y, "gy", axis=0, tiled=True)
    pieces = lax.all_to_all(outbox_x, "gx", 0, 0, tiled=True)
    first, second, more = pl.pallas_call(
        sort_kernel,
        out_shape=[struct(count_x, PIECE, 128)] * 2 + [struct(1, dtype=jnp.int32)],
        in_specs=[spec(VMEM)],
        out_specs=[spec(VMEM)] * 2 + [spec(SMEM)],
        scratch_shapes=[SMEM((count_x,), jnp.int32)],
        compiler_params=PARAMS,
        name="sort",
    )(pieces)
    first = lax.all_to_all(first, "gx", 0, 0, tiled=True)
    second = lax.cond(
        more[0] > 0,
        lambda value: lax.all_to_all(value, "gx", 0, 0, tiled=True),
        lambda value: value,
        second,
    )
    state, *planes = pl.pallas_call(
        functools.partial(place_kernel, count_y),
        out_shape=[struct(ROWS, 128)] + PLANES,
        in_specs=[spec(SMEM)] * 2 + [spec(pl.ANY)] * 4,
        out_specs=[spec(VMEM)] * 5,
        scratch_shapes=[
            VMEM((2, TAG, 128), F32),
            VMEM((count_y, TAG, 128), F32),
            pltpu.SemaphoreType.DMA((3,)),
            pltpu.SemaphoreType.DMA((SLOTS,)),
        ],
        compiler_params=PARAMS,
        name="place",
    )(new_owner, new_slot, boxes, first, second, all_y)
    constants = (diffusivity, stoichiometry, heat_release, prefactor, activation)
    for step_index in range(STEPS):
        x_a, x_b, y_a, y_b = planes
        received = (swapped(x_a, "gx", 0), swapped(x_b, "gx", 1), swapped(y_a, "gy", 0), swapped(y_b, "gy", 1))
        if step_index < STEPS - 1:
            state, *planes = step(False, neighbours, constants, state, received)
        else:
            state = step(True, neighbours, constants, state, received)
    return state.reshape(COMPS, 128, SLOTS, 128).transpose(2, 0, 1, 3).reshape(SLOTS, COMPS, BZ * BX * BX)


def solution(mesh):
    return jax.shard_map(
        shards,
        mesh=mesh,
        in_specs=(
            P(("gx", "gy"), None, None),
            P(("gx", "gy")),
            P(("gx", "gy")),
            P(("gx", "gy"), None),
            P(),
            P(),
            P(),
            P(),
            P(),
        ),
        out_specs=P(("gx", "gy"), None, None),
        check_vma=False,
    )
```

```python
import functools

import jax
import jax.numpy as jnp
from jax import lax
from jax.experimental import pallas as pl
from jax.experimental.pallas import tpu as pltpu
from jax.sharding import PartitionSpec as P

NSPEC = 9
COMPS = 13
TEMP = 12
BX = 32
BZ = 16
SLOTS = 2
STEPS = 3
LAYERS = SLOTS * BZ
LROWS = COMPS * 8
BROWS = BZ * LROWS
ROWS = SLOTS * BROWS
TAG = 8
PIECE = LROWS + TAG
YBOX = BROWS + TAG
NONE = -1.0
SMEM = pltpu.SMEM
VMEM = pltpu.VMEM
F32 = jnp.float32
PARAMS = pltpu.CompilerParams(vmem_limit_bytes=48 * 1024 * 1024)


def swapped(value, axis, first):
    count = lax.axis_size(axis)
    pairs = []
    for low in range(first, count + first, 2):
        pairs += [(low % count, (low + 1) % count), ((low + 1) % count, low % count)]
    return lax.ppermute(value, axis, pairs)


def moves(target_ref, row, count_y, index_x, index_y):
    slot = lax.rem(target_ref[row], SLOTS)
    owner = target_ref[row] // SLOTS
    dest_x = owner // count_y
    dest_y = owner - dest_x * count_y
    goes_x = (dest_y == index_y) & (dest_x != index_x)
    goes_y = (dest_x == index_x) & (dest_y != index_y)
    return dest_x, dest_y, slot, goes_x, goes_y


def source_rows(n, z, c):
    return pl.ds(c * 256 + z * 16 + n, 8, stride=2)


def pack_kernel(count_y, target_ref, old_ref, box_ref, outx_ref, outy_ref):
    index_x = lax.axis_index("gx")
    index_y = lax.axis_index("gy")
    row_x = jnp.int32(0)
    row_y = jnp.int32(0)
    tag_x = jnp.int32(-1)
    tag_y = jnp.int32(-1)
    for n in range(SLOTS):
        dest_x, dest_y, slot, goes_x, goes_y = moves(target_ref, n, count_y, index_x, index_y)
        row_x = jnp.where(goes_x, n, row_x)
        row_y = jnp.where(goes_y, n, row_y)
        tag_x = jnp.where(goes_x, dest_x * SLOTS + slot, tag_x)
        tag_y = jnp.where(goes_y, dest_y * SLOTS + slot, tag_y)
    first_x = jnp.full((8, 128), row_x, jnp.int32) == 0
    first_y = jnp.full((8, 128), row_y, jnp.int32) == 0

    def layer(z, carry):
        row = pl.multiple_of(z * LROWS, 8)
        for c in range(COMPS):
            zero = old_ref[source_rows(0, z, c), :]
            one = old_ref[source_rows(1, z, c), :]
            box_ref[pl.ds(row + c * 8, 8), :] = zero
            box_ref[pl.ds(BROWS + row + c * 8, 8), :] = one
            outx_ref[z, c * 8 : c * 8 + 8, :] = jnp.where(first_x, zero, one)
            outy_ref[0, pl.ds(row + c * 8, 8), :] = jnp.where(first_y, zero, one)
        outx_ref[z, LROWS:, :] = jnp.full((TAG, 128), tag_x, jnp.int32).astype(F32)
        return carry

    lax.fori_loop(0, BZ, layer, 0)
    outy_ref[0, BROWS:, :] = jnp.full((TAG, 128), tag_y, jnp.int32).astype(F32)


def tag_of(tile):
    return jnp.max(tile).astype(jnp.int32)


def sort_kernel(pieces_ref, first_ref, second_ref, more_ref, used_ref):
    count = pieces_ref.shape[0]
    empty = jnp.full((TAG, 128), NONE, F32)
    more_ref[0] = 0
    tags = []
    for d in range(count):
        first_ref[d, LROWS:, :] = empty
        second_ref[d, LROWS:, :] = empty
        used_ref[d] = 0
        tags.append(tag_of(pieces_ref[d, LROWS:, :]))
    for s in range(count):
        tag = tags[s]
        there = jnp.maximum(tag, 0) // SLOTS
        used = used_ref[there]

        @pl.when((tag >= 0) & (used == 0))
        def _():
            first_ref[there, :, :] = pieces_ref[s]
            used_ref[there] = 1

        @pl.when((tag >= 0) & (used == 1))
        def _():
            second_ref[there, :, :] = pieces_ref[s]
            more_ref[0] = 1


def roll(value, shift, axis):
    if isinstance(shift, int):
        shift = shift % value.shape[axis]
        if shift == 0:
            return value
        return pltpu.roll(value, shift, axis)
    return pltpu.roll(value, lax.rem(shift + 256, 128), axis)


def lanes():
    return lax.broadcasted_iota(jnp.int32, (8, 128), 1)


def sublanes():
    return lax.broadcasted_iota(jnp.int32, (8, 128), 0)


def tile(row):
    return pl.ds(pl.multiple_of(row, 8), 8)


def put_faces(value_of, state_ref, out_refs):
    lane = lanes()
    ends = ((lane & 31) == 0) | ((lane & 31) == 31)
    even = (lane & 1) == 0
    group = lane >> 5
    even_x = lax.rem(lax.axis_index("gx"), 2) == 0
    even_y = lax.rem(lax.axis_index("gy"), 2) == 0
    xa_ref, xb_ref, ya_ref, yb_ref = out_refs

    for c in range(COMPS):
        rows = pl.ds(c * 8, 8)
        both = []
        for n in range(SLOTS):
            parts = [roll(jnp.where(ends, value_of(n, z, c), 0.0), 2 * z, 1) for z in range(BZ)]
            while len(parts) > 1:
                parts = [a + b for a, b in zip(parts[::2], parts[1::2])]
            both.append(parts[0])
        other = roll(both[1], 1, 1)
        low = jnp.where(even, both[0], other)
        high = jnp.where(even, other, both[0])
        xa_ref[rows, :] = jnp.where(even_x, high, low)
        xb_ref[rows, :] = jnp.where(even_x, low, high)
        low = jnp.zeros((8, 128), F32)
        high = jnp.zeros((8, 128), F32)
        for n in range(SLOTS):
            for half in range(2):
                where = 2 * n + half
                base = n * BROWS + half * 8 * LROWS + c * 8
                bottom = state_ref[pl.ds(base, 8, stride=LROWS), :]
                top = state_ref[pl.ds(base + 7, 8, stride=LROWS), :]
                low = jnp.where(group == where, roll(bottom, 32 * where, 1), low)
                high = jnp.where(group == where, roll(top, 32 * where - 96, 1), high)
        ya_ref[rows, :] = jnp.where(even_y, high, low)
        yb_ref[rows, :] = jnp.where(even_y, low, high)


def into(state_ref, slot):
    return state_ref.at[pl.ds(pl.multiple_of(slot * BROWS, 8), BROWS), :]


def place_kernel(count_y, target_ref, box_ref, first_ref, second_ref, state_ref, sems):
    index_x = lax.axis_index("gx")
    index_y = lax.axis_index("gy")
    for n in range(SLOTS):
        dest_x, dest_y, slot, goes_x, goes_y = moves(target_ref, n, count_y, index_x, index_y)

        @pl.when((dest_x == index_x) & (dest_y == index_y))
        def _():
            load = pltpu.make_async_copy(
                box_ref.at[pl.ds(n * BROWS, BROWS), :], into(state_ref, slot), sems.at[0]
            )
            load.start()
            load.wait()

    for source in (first_ref, second_ref):
        tag = tag_of(source[0, LROWS:, :])

        @pl.when(tag >= 0)
        def _():
            base = lax.rem(tag, SLOTS) * BROWS
            loads = [
                pltpu.make_async_copy(
                    source.at[z, pl.ds(0, LROWS), :],
                    state_ref.at[pl.ds(pl.multiple_of(base + z * LROWS, 8), LROWS), :],
                    sems.at[z],
                )
                for z in range(BZ)
            ]
            for load in loads:
                load.start()
            for load in loads:
                load.wait()


def place_y_kernel(_, ally_ref, state_ref, xa_ref, xb_ref, ya_ref, yb_ref, tag_ref, sem):
    index_y = lax.axis_index("gy")
    load = pltpu.make_async_copy(ally_ref.at[:, pl.ds(BROWS, TAG), :], tag_ref, sem)
    load.start()
    load.wait()
    for p in range(tag_ref.shape[0]):
        tag = tag_of(tag_ref[p])

        @pl.when((tag >= 0) & (tag // SLOTS == index_y))
        def _():
            box = pltpu.make_async_copy(
                ally_ref.at[p, pl.ds(0, BROWS), :], into(state_ref, lax.rem(tag, SLOTS)), sem
            )
            box.start()
            box.wait()

    put_faces(
        lambda n, z, c: state_ref[pl.ds((n * BZ + z) * LROWS + c * 8, 8), :],
        state_ref,
        (xa_ref, xb_ref, ya_ref, yb_ref),
    )


def power(value):
    return jnp.exp(0.7 * jnp.log(value))


UNROLL = 4


def inside_kernel(near_ref, diff_ref, stoi_ref, heat_ref, pre_ref, act_ref, state_ref, new_ref, coef_ref):
    lane = lanes()
    sub = sublanes()
    y_low_lanes = lane < 32
    y_high_lanes = lane >= 96
    inner = [
        (lane & 31) != 0,
        (lane & 31) != 31,
        ~(y_low_lanes & (sub == 0)),
        ~(y_high_lanes & (sub == 7)),
    ]

    def power_layer(block, carry):
        for u in range(8):
            index = block * 8 + u
            coef_ref[tile(index * 8), :] = power(state_ref[tile(index * LROWS + TEMP * 8), :])
        return carry

    lax.fori_loop(0, LAYERS // 8, power_layer, 0)

    def layer(n, z):
        index = n * BZ + z
        near_zm = near_ref[n, 4]
        near_zp = near_ref[n, 5]
        index_m = jnp.where(z == 0, jnp.where(near_zm < 0, index, near_zm * BZ + BZ - 1), index - 1)
        index_p = jnp.where(z == BZ - 1, jnp.where(near_zp < 0, index, near_zp * BZ), index + 1)

        def beside(value):
            down = roll(value, 32, 1)
            up = roll(value, -32, 1)
            return (
                roll(value, 1, 1),
                roll(value, -1, 1),
                jnp.where(y_low_lanes, roll(down, 1, 0), down),
                jnp.where(y_high_lanes, roll(up, -1, 0), up),
            )

        center = coef_ref[tile(index * 8), :]
        weights = [
            jnp.where(mask, 0.5 * (center + side), 0.0) for mask, side in zip(inner, beside(center))
        ]
        for at in (index_m, index_p):
            weights.append(0.5 * (center + coef_ref[tile(at * 8), :]))
        total = functools.reduce(lambda a, b: a + b, weights)
        row = pl.multiple_of(index * LROWS, 8)
        row_m = pl.multiple_of(index_m * LROWS, 8)
        row_p = pl.multiple_of(index_p * LROWS, 8)
        rate = (
            pre_ref[0]
            * state_ref[pl.ds(row, 8), :]
            * state_ref[pl.ds(row + 8, 8), :]
            * jnp.exp(-act_ref[0] / state_ref[pl.ds(row + TEMP * 8, 8), :])
        )
        for c in range(COMPS):
            value = state_ref[pl.ds(row + c * 8, 8), :]
            sides = beside(value)
            sides = sides + (state_ref[pl.ds(row_m + c * 8, 8), :], state_ref[pl.ds(row_p + c * 8, 8), :])
            change = -total * value
            for weight, side in zip(weights, sides):
                change = change + weight * side
            value = value + diff_ref[c] * change
            if c < NSPEC:
                value = value + stoi_ref[c] * rate
            elif c == TEMP:
                value = value + heat_ref[0] * rate
            new_ref[pl.ds(row + c * 8, 8), :] = value

    def layers(block, carry):
        n = block // (BZ // UNROLL)
        z = (block - n * (BZ // UNROLL)) * UNROLL
        for u in range(UNROLL):
            layer(n, z + u)
        return carry

    lax.fori_loop(0, LAYERS // UNROLL, layers, 0)


def ghost_kernel(last, near_ref, diff_ref, part_ref, *refs):
    own_refs, got_refs, (new_ref, *out_refs, ym_ref, yp_ref) = refs[:4], refs[4:8], refs[8:]
    lane = lanes()
    even = (lane & 1) == 0
    ends = ((lane & 31) == 0) | ((lane & 31) == 31)
    first_box = lane < 64
    y_first = (lane < 32) & (sublanes() == 0)
    y_last = (lane >= 96) & (sublanes() == 7)
    even_x = lax.rem(lax.axis_index("gx"), 2) == 0
    even_y = lax.rem(lax.axis_index("gy"), 2) == 0

    def plane_pairs(c):
        rows = slice(c * 8, c * 8 + 8)
        own_a, own_b, own_ya, own_yb = (ref[rows, :] for ref in own_refs)
        got_a, got_b, got_ya, got_yb = (ref[rows, :] for ref in got_refs)
        low = jnp.where(even_x, own_b, own_a)
        high = jnp.where(even_x, own_a, own_b)
        below = jnp.where(even_x, got_b, got_a)
        above = jnp.where(even_x, got_a, got_b)
        own = (jnp.where(even, low, high), roll(jnp.where(even, high, low), -1, 1))
        pairs = []
        for n in range(SLOTS):
            ghost = jnp.where(
                even, roll(below, -31 - near_ref[n, 0], 1), roll(above, 31 - near_ref[n, 1], 1)
            )
            pairs.append((own[n], ghost))
        low = jnp.where(even_y, own_yb, own_ya)
        high = jnp.where(even_y, own_ya, own_yb)
        below = jnp.where(even_y, got_yb, got_ya)
        above = jnp.where(even_y, got_ya, got_yb)
        for side, mine, theirs in ((2, low, below), (3, high, above)):
            other = roll(theirs, 64, 1)
            ghost = jnp.where(
                first_box,
                jnp.where(near_ref[0, side] == 0, theirs, other),
                jnp.where(near_ref[1, side] == 1, theirs, other),
            )
            pairs.append((mine, ghost))
        return pairs

    weights = [0.5 * (power(own) + power(ghost)) for own, ghost in plane_pairs(TEMP)]
    x_terms = []
    for c in range(COMPS):
        terms = [
            diff_ref[c] * (weight * (ghost - own)) for weight, (own, ghost) in zip(weights, plane_pairs(c))
        ]
        x_terms.append(terms[:SLOTS])
        for n in range(SLOTS):
            for half in range(2):
                where = 32 * (2 * n + half)
                rows = pl.ds((c * SLOTS + n) * BZ + half * 8, 8)
                ym_ref[rows, :] = roll(terms[2], -where, 1)
                yp_ref[rows, :] = roll(terms[3], 96 - where, 1)

    def value_of(n, z, c):
        row = (n * BZ + z) * LROWS + c * 8
        at = pl.ds((c * SLOTS + n) * BZ + z, 1)
        value = part_ref[pl.ds(row, 8), :] + jnp.where(ends, roll(x_terms[c][n], -2 * z, 1), 0.0)
        low = jnp.broadcast_to(ym_ref[at, :], (8, 128))
        high = jnp.broadcast_to(yp_ref[at, :], (8, 128))
        value = value + jnp.where(y_first, low, jnp.where(y_last, high, 0.0))
        if last:
            new_ref[source_rows(n, z, c), :] = value
        else:
            new_ref[pl.ds(row, 8), :] = value
        return value

    if last:
        for c in range(COMPS):
            for n in range(SLOTS):
                for z in range(BZ):
                    value_of(n, z, c)
    else:
        put_faces(value_of, new_ref, out_refs)


def spec(space):
    return pl.BlockSpec(memory_space=space)


def struct(*shape, dtype=F32):
    return jax.ShapeDtypeStruct(shape, dtype)


PLANES = [struct(LROWS, 128)] * 4


def inside(near, constants, state):
    return pl.pallas_call(
        inside_kernel,
        out_shape=struct(ROWS, 128),
        in_specs=[spec(SMEM)] * 6 + [spec(VMEM)],
        out_specs=spec(VMEM),
        scratch_shapes=[VMEM((LAYERS * 8, 128), F32)],
        compiler_params=PARAMS,
        cost_estimate=pl.CostEstimate(flops=20_000_000, bytes_accessed=4_000_000, transcendentals=0),
        name="inside",
    )(near, *constants, state)


def add_ghosts(last, near, diffusivity, part, sent, received):
    out_shape = struct(ROWS, 128) if last else [struct(ROWS, 128)] + PLANES
    out_specs = spec(VMEM) if last else [spec(VMEM)] * 5
    return pl.pallas_call(
        functools.partial(ghost_kernel, last),
        out_shape=out_shape,
        in_specs=[spec(SMEM)] * 2 + [spec(VMEM)] * 9,
        out_specs=out_specs,
        scratch_shapes=[VMEM((COMPS * SLOTS * BZ, 128), F32)] * 2,
        compiler_params=PARAMS,
        name="ghosts_last" if last else "ghosts",
    )(near, diffusivity, part, *sent, *received)


def shards(
    old_state,
    new_owner,
    new_slot,
    neighbours,
    diffusivity,
    stoichiometry,
    heat_release,
    prefactor,
    activation,
):
    count_x = lax.axis_size("gx")
    count_y = lax.axis_size("gy")
    target = new_owner * SLOTS + new_slot
    old_rows = old_state.reshape(SLOTS, COMPS, 128, 128).transpose(1, 2, 0, 3).reshape(ROWS, 128)
    boxes, outbox_x, outbox_y = pl.pallas_call(
        functools.partial(pack_kernel, count_y),
        out_shape=[struct(ROWS, 128), struct(BZ, PIECE, 128), struct(1, YBOX, 128)],
        in_specs=[spec(SMEM), spec(VMEM)],
        out_specs=[spec(VMEM)] * 3,
        compiler_params=PARAMS,
        name="pack",
    )(target, old_rows)
    all_y = lax.all_gather(outbox_y, "gy", axis=0, tiled=True)
    pieces = lax.all_to_all(outbox_x, "gx", 0, 0, tiled=True)
    first, second, more = pl.pallas_call(
        sort_kernel,
        out_shape=[struct(count_x, PIECE, 128)] * 2 + [struct(1, dtype=jnp.int32)],
        in_specs=[spec(VMEM)],
        out_specs=[spec(VMEM)] * 2 + [spec(SMEM)],
        scratch_shapes=[SMEM((count_x,), jnp.int32)],
        compiler_params=PARAMS,
        name="sort",
    )(pieces)
    first = lax.all_to_all(first, "gx", 0, 0, tiled=True)
    second = lax.cond(
        more[0] > 0,
        lambda value: lax.all_to_all(value, "gx", 0, 0, tiled=True),
        lambda value: value,
        second,
    )
    state = pl.pallas_call(
        functools.partial(place_kernel, count_y),
        out_shape=struct(ROWS, 128),
        in_specs=[spec(SMEM)] + [spec(VMEM)] * 3,
        out_specs=spec(VMEM),
        scratch_shapes=[pltpu.SemaphoreType.DMA((BZ,))],
        compiler_params=PARAMS,
        name="place",
    )(target, boxes, first, second)
    state, *planes = pl.pallas_call(
        place_y_kernel,
        out_shape=[struct(ROWS, 128)] + PLANES,
        in_specs=[spec(VMEM), spec(pl.ANY)],
        out_specs=[spec(VMEM)] * 5,
        input_output_aliases={0: 0},
        scratch_shapes=[VMEM((count_y, TAG, 128), F32), pltpu.SemaphoreType.DMA],
        compiler_params=PARAMS,
        name="place_y",
    )(state, all_y)
    constants = (diffusivity, stoichiometry, heat_release, prefactor, activation)
    for step_index in range(STEPS):
        x_a, x_b, y_a, y_b = planes
        received = (swapped(x_a, "gx", 0), swapped(x_b, "gx", 1), swapped(y_a, "gy", 0), swapped(y_b, "gy", 1))
        part = inside(neighbours, constants, state)
        if step_index < STEPS - 1:
            state, *planes = add_ghosts(False, neighbours, diffusivity, part, planes, received)
        else:
            state = add_ghosts(True, neighbours, diffusivity, part, planes, received)
    return state.reshape(COMPS, 128, SLOTS, 128).transpose(2, 0, 1, 3).reshape(SLOTS, COMPS, BZ * BX * BX)


def solution(mesh):
    return jax.shard_map(
        shards,
        mesh=mesh,
        in_specs=(
            P(("gx", "gy"), None, None),
            P(("gx", "gy")),
            P(("gx", "gy")),
            P(("gx", "gy"), None),
            P(),
            P(),
            P(),
            P(),
            P(),
        ),
        out_specs=P(("gx", "gy"), None, None),
        check_vma=False,
    )
```

```python
import functools

import jax
import jax.numpy as jnp
from jax import lax
from jax.experimental import pallas as pl
from jax.experimental.pallas import tpu as pltpu
from jax.sharding import PartitionSpec as P

NSPEC = 9
COMPS = 13
TEMP = 12
BX = 32
BZ = 16
SLOTS = 2
STEPS = 3
LAYERS = SLOTS * BZ
LROWS = COMPS * 8
BROWS = BZ * LROWS
ROWS = SLOTS * BROWS
TAG = 8
PIECE = LROWS + TAG
YBOX = BROWS + TAG
NONE = -1.0
SMEM = pltpu.SMEM
VMEM = pltpu.VMEM
F32 = jnp.float32
PARAMS = pltpu.CompilerParams(vmem_limit_bytes=48 * 1024 * 1024)


def swapped(value, axis, first):
    count = lax.axis_size(axis)
    pairs = []
    for low in range(first, count + first, 2):
        pairs += [(low % count, (low + 1) % count), ((low + 1) % count, low % count)]
    return lax.ppermute(value, axis, pairs)


def moves(target_ref, row, count_y, index_x, index_y):
    slot = lax.rem(target_ref[row], SLOTS)
    owner = target_ref[row] // SLOTS
    dest_x = owner // count_y
    dest_y = owner - dest_x * count_y
    goes_x = (dest_y == index_y) & (dest_x != index_x)
    goes_y = (dest_x == index_x) & (dest_y != index_y)
    return dest_x, dest_y, slot, goes_x, goes_y


def source_rows(n, z, c):
    return pl.ds(c * 256 + z * 16 + n, 8, stride=2)


def pack_kernel(count_y, target_ref, old_ref, box_ref, outx_ref, outy_ref):
    index_x = lax.axis_index("gx")
    index_y = lax.axis_index("gy")
    row_x = jnp.int32(0)
    row_y = jnp.int32(0)
    tag_x = jnp.int32(-1)
    tag_y = jnp.int32(-1)
    for n in range(SLOTS):
        dest_x, dest_y, slot, goes_x, goes_y = moves(target_ref, n, count_y, index_x, index_y)
        row_x = jnp.where(goes_x, n, row_x)
        row_y = jnp.where(goes_y, n, row_y)
        tag_x = jnp.where(goes_x, dest_x * SLOTS + slot, tag_x)
        tag_y = jnp.where(goes_y, dest_y * SLOTS + slot, tag_y)
    first_x = jnp.full((8, 128), row_x, jnp.int32) == 0
    first_y = jnp.full((8, 128), row_y, jnp.int32) == 0

    def layer(z, carry):
        row = pl.multiple_of(z * LROWS, 8)
        for c in range(COMPS):
            zero = old_ref[source_rows(0, z, c), :]
            one = old_ref[source_rows(1, z, c), :]
            box_ref[pl.ds(row + c * 8, 8), :] = zero
            box_ref[pl.ds(BROWS + row + c * 8, 8), :] = one
            outx_ref[z, c * 8 : c * 8 + 8, :] = jnp.where(first_x, zero, one)
            outy_ref[0, pl.ds(row + c * 8, 8), :] = jnp.where(first_y, zero, one)
        outx_ref[z, LROWS:, :] = jnp.full((TAG, 128), tag_x, jnp.int32).astype(F32)
        return carry

    lax.fori_loop(0, BZ, layer, 0)
    outy_ref[0, BROWS:, :] = jnp.full((TAG, 128), tag_y, jnp.int32).astype(F32)


def tag_of(tile):
    return jnp.max(tile).astype(jnp.int32)


def sort_kernel(pieces_ref, first_ref, second_ref, more_ref, used_ref):
    count = pieces_ref.shape[0]
    empty = jnp.full((TAG, 128), NONE, F32)
    more_ref[0] = 0
    tags = []
    for d in range(count):
        first_ref[d, LROWS:, :] = empty
        second_ref[d, LROWS:, :] = empty
        used_ref[d] = 0
        tags.append(tag_of(pieces_ref[d, LROWS:, :]))
    for s in range(count):
        tag = tags[s]
        there = jnp.maximum(tag, 0) // SLOTS
        used = used_ref[there]

        @pl.when((tag >= 0) & (used == 0))
        def _():
            first_ref[there, :, :] = pieces_ref[s]
            used_ref[there] = 1

        @pl.when((tag >= 0) & (used == 1))
        def _():
            second_ref[there, :, :] = pieces_ref[s]
            more_ref[0] = 1


def roll(value, shift, axis):
    if isinstance(shift, int):
        shift = shift % value.shape[axis]
        if shift == 0:
            return value
        return pltpu.roll(value, shift, axis)
    return pltpu.roll(value, lax.rem(shift + 256, 128), axis)


def lanes():
    return lax.broadcasted_iota(jnp.int32, (8, 128), 1)


def sublanes():
    return lax.broadcasted_iota(jnp.int32, (8, 128), 0)


def tile(row):
    return pl.ds(pl.multiple_of(row, 8), 8)


def put_faces(value_of, state_ref, out_refs):
    lane = lanes()
    ends = ((lane & 31) == 0) | ((lane & 31) == 31)
    even = (lane & 1) == 0
    group = lane >> 5
    even_x = lax.rem(lax.axis_index("gx"), 2) == 0
    even_y = lax.rem(lax.axis_index("gy"), 2) == 0
    xa_ref, xb_ref, ya_ref, yb_ref = out_refs

    for c in range(COMPS):
        rows = pl.ds(c * 8, 8)
        both = []
        for n in range(SLOTS):
            parts = [roll(jnp.where(ends, value_of(n, z, c), 0.0), 2 * z, 1) for z in range(BZ)]
            while len(parts) > 1:
                parts = [a + b for a, b in zip(parts[::2], parts[1::2])]
            both.append(parts[0])
        other = roll(both[1], 1, 1)
        low = jnp.where(even, both[0], other)
        high = jnp.where(even, other, both[0])
        xa_ref[rows, :] = jnp.where(even_x, high, low)
        xb_ref[rows, :] = jnp.where(even_x, low, high)
        low = jnp.zeros((8, 128), F32)
        high = jnp.zeros((8, 128), F32)
        for n in range(SLOTS):
            for half in range(2):
                where = 2 * n + half
                base = n * BROWS + half * 8 * LROWS + c * 8
                bottom = state_ref[pl.ds(base, 8, stride=LROWS), :]
                top = state_ref[pl.ds(base + 7, 8, stride=LROWS), :]
                low = jnp.where(group == where, roll(bottom, 32 * where, 1), low)
                high = jnp.where(group == where, roll(top, 32 * where - 96, 1), high)
        ya_ref[rows, :] = jnp.where(even_y, high, low)
        yb_ref[rows, :] = jnp.where(even_y, low, high)


def place_kernel(count_y, target_ref, box_ref, first_ref, second_ref, state_ref):
    index_x = lax.axis_index("gx")
    index_y = lax.axis_index("gy")
    tags = [tag_of(source[0, LROWS:, :]) for source in (first_ref, second_ref)]

    def put(slot, z, value):
        state_ref[pl.ds(pl.multiple_of(slot * BROWS + z * LROWS, 8), LROWS), :] = value

    for n in range(SLOTS):
        dest_x, dest_y, slot, goes_x, goes_y = moves(target_ref, n, count_y, index_x, index_y)

        @pl.when((dest_x == index_x) & (dest_y == index_y))
        def _():
            for z in range(BZ):
                put(slot, z, box_ref[pl.ds(n * BROWS + z * LROWS, LROWS), :])

    for tag, source in zip(tags, (first_ref, second_ref)):

        @pl.when(tag >= 0)
        def _():
            for z in range(BZ):
                put(lax.rem(tag, SLOTS), z, source[z, :LROWS, :])


def place_y_kernel(_, ally_ref, state_ref, xa_ref, xb_ref, ya_ref, yb_ref, tag_ref, tag_sem, sems):
    load = pltpu.make_async_copy(ally_ref.at[:, pl.ds(BROWS, TAG), :], tag_ref, tag_sem)
    load.start()
    index_y = jnp.full((TAG, 128), lax.axis_index("gy"), jnp.int32)
    load.wait()
    places = []
    for slot in range(SLOTS):
        wanted = (index_y * SLOTS + slot).astype(F32)
        hits = [jnp.where(tag_ref[p] == wanted, p + 1.0, 0.0) for p in range(tag_ref.shape[0])]
        places.append(tag_of(functools.reduce(jnp.maximum, hits)))
    boxes = [
        pltpu.make_async_copy(
            ally_ref.at[jnp.maximum(place - 1, 0), pl.ds(0, BROWS), :],
            state_ref.at[pl.ds(slot * BROWS, BROWS), :],
            sems.at[slot],
        )
        for slot, place in enumerate(places)
    ]
    for place, box in zip(places, boxes):

        @pl.when(place > 0)
        def _():
            box.start()

    for place, box in zip(places, boxes):

        @pl.when(place > 0)
        def _():
            box.wait()

    put_faces(
        lambda n, z, c: state_ref[pl.ds((n * BZ + z) * LROWS + c * 8, 8), :],
        state_ref,
        (xa_ref, xb_ref, ya_ref, yb_ref),
    )


def power(value):
    return jnp.exp(0.7 * jnp.log(value))


UNROLL = 8


def inside_kernel(near_ref, diff_ref, stoi_ref, heat_ref, pre_ref, act_ref, state_ref, new_ref, coef_ref):
    lane = lanes()
    sub = sublanes()
    y_low_lanes = lane < 32
    y_high_lanes = lane >= 96
    inner = [
        (lane & 31) != 0,
        (lane & 31) != 31,
        ~(y_low_lanes & (sub == 0)),
        ~(y_high_lanes & (sub == 7)),
    ]

    def power_layer(block, carry):
        for u in range(8):
            index = block * 8 + u
            coef_ref[tile(index * 8), :] = power(state_ref[tile(index * LROWS + TEMP * 8), :])
        return carry

    lax.fori_loop(0, LAYERS // 8, power_layer, 0)

    def layer(n, z):
        index = n * BZ + z
        near_zm = near_ref[n, 4]
        near_zp = near_ref[n, 5]
        index_m = jnp.where(z == 0, jnp.where(near_zm < 0, index, near_zm * BZ + BZ - 1), index - 1)
        index_p = jnp.where(z == BZ - 1, jnp.where(near_zp < 0, index, near_zp * BZ), index + 1)

        def beside(value):
            down = roll(value, 32, 1)
            up = roll(value, -32, 1)
            return (
                roll(value, 1, 1),
                roll(value, -1, 1),
                jnp.where(y_low_lanes, roll(down, 1, 0), down),
                jnp.where(y_high_lanes, roll(up, -1, 0), up),
            )

        center = coef_ref[tile(index * 8), :]
        weights = [
            jnp.where(mask, 0.5 * (center + side), 0.0) for mask, side in zip(inner, beside(center))
        ]
        for at in (index_m, index_p):
            weights.append(0.5 * (center + coef_ref[tile(at * 8), :]))
        total = functools.reduce(lambda a, b: a + b, weights)
        row = pl.multiple_of(index * LROWS, 8)
        row_m = pl.multiple_of(index_m * LROWS, 8)
        row_p = pl.multiple_of(index_p * LROWS, 8)
        rate = (
            pre_ref[0]
            * state_ref[pl.ds(row, 8), :]
            * state_ref[pl.ds(row + 8, 8), :]
            * jnp.exp(-act_ref[0] / state_ref[pl.ds(row + TEMP * 8, 8), :])
        )
        for c in range(COMPS):
            value = state_ref[pl.ds(row + c * 8, 8), :]
            sides = beside(value)
            sides = sides + (state_ref[pl.ds(row_m + c * 8, 8), :], state_ref[pl.ds(row_p + c * 8, 8), :])
            change = -total * value
            for weight, side in zip(weights, sides):
                change = change + weight * side
            value = value + diff_ref[c] * change
            if c < NSPEC:
                value = value + stoi_ref[c] * rate
            elif c == TEMP:
                value = value + heat_ref[0] * rate
            new_ref[pl.ds(row + c * 8, 8), :] = value

    def layers(block, carry):
        n = block // (BZ // UNROLL)
        z = (block - n * (BZ // UNROLL)) * UNROLL
        for u in range(UNROLL):
            layer(n, z + u)
        return carry

    lax.fori_loop(0, LAYERS // UNROLL, layers, 0)


def ghost_kernel(last, near_ref, diff_ref, part_ref, *refs):
    own_refs, got_refs = refs[:4], refs[4:8]
    if last:
        out_ref, ym_ref, yp_ref, new_ref, sems = refs[8:]
    else:
        new_ref, *out_refs, ym_ref, yp_ref = refs[8:]
    lane = lanes()
    even = (lane & 1) == 0
    ends = ((lane & 31) == 0) | ((lane & 31) == 31)
    first_box = lane < 64
    y_first = (lane < 32) & (sublanes() == 0)
    y_last = (lane >= 96) & (sublanes() == 7)
    even_x = lax.rem(lax.axis_index("gx"), 2) == 0
    even_y = lax.rem(lax.axis_index("gy"), 2) == 0

    def plane_pairs(c):
        rows = slice(c * 8, c * 8 + 8)
        own_a, own_b, own_ya, own_yb = (ref[rows, :] for ref in own_refs)
        got_a, got_b, got_ya, got_yb = (ref[rows, :] for ref in got_refs)
        low = jnp.where(even_x, own_b, own_a)
        high = jnp.where(even_x, own_a, own_b)
        below = jnp.where(even_x, got_b, got_a)
        above = jnp.where(even_x, got_a, got_b)
        own = (jnp.where(even, low, high), roll(jnp.where(even, high, low), -1, 1))
        pairs = []
        for n in range(SLOTS):
            ghost = jnp.where(
                even, roll(below, -31 - near_ref[n, 0], 1), roll(above, 31 - near_ref[n, 1], 1)
            )
            pairs.append((own[n], ghost))
        low = jnp.where(even_y, own_yb, own_ya)
        high = jnp.where(even_y, own_ya, own_yb)
        below = jnp.where(even_y, got_yb, got_ya)
        above = jnp.where(even_y, got_ya, got_yb)
        for side, mine, theirs in ((2, low, below), (3, high, above)):
            other = roll(theirs, 64, 1)
            ghost = jnp.where(
                first_box,
                jnp.where(near_ref[0, side] == 0, theirs, other),
                jnp.where(near_ref[1, side] == 1, theirs, other),
            )
            pairs.append((mine, ghost))
        return pairs

    weights = [0.5 * (power(own) + power(ghost)) for own, ghost in plane_pairs(TEMP)]
    x_terms = []
    for c in range(COMPS):
        terms = [
            diff_ref[c] * (weight * (ghost - own)) for weight, (own, ghost) in zip(weights, plane_pairs(c))
        ]
        x_terms.append(terms[:SLOTS])
        for n in range(SLOTS):
            for half in range(2):
                where = 32 * (2 * n + half)
                rows = pl.ds((c * SLOTS + n) * BZ + half * 8, 8)
                ym_ref[rows, :] = roll(terms[2], -where, 1)
                yp_ref[rows, :] = roll(terms[3], 96 - where, 1)

    def value_of(n, z, c):
        row = (n * BZ + z) * LROWS + c * 8
        at = pl.ds((c * SLOTS + n) * BZ + z, 1)
        value = part_ref[pl.ds(row, 8), :] + jnp.where(ends, roll(x_terms[c][n], -2 * z, 1), 0.0)
        low = jnp.broadcast_to(ym_ref[at, :], (8, 128))
        high = jnp.broadcast_to(yp_ref[at, :], (8, 128))
        value = value + jnp.where(y_first, low, jnp.where(y_last, high, 0.0))
        if last:
            new_ref[source_rows(n, z, c), :] = value
        else:
            new_ref[pl.ds(row, 8), :] = value
        return value

    if last:
        stores = []
        for c in range(COMPS):
            for n in range(SLOTS):
                for z in range(BZ):
                    value_of(n, z, c)
            rows = pl.ds(c * 256, 256)
            stores.append(pltpu.make_async_copy(new_ref.at[rows, :], out_ref.at[rows, :], sems.at[c]))
            stores[c].start()
        for store in stores:
            store.wait()
    else:
        put_faces(value_of, new_ref, out_refs)


def spec(space):
    return pl.BlockSpec(memory_space=space)


def struct(*shape, dtype=F32):
    return jax.ShapeDtypeStruct(shape, dtype)


PLANES = [struct(LROWS, 128)] * 4


def inside(near, constants, state):
    return pl.pallas_call(
        inside_kernel,
        out_shape=struct(ROWS, 128),
        in_specs=[spec(SMEM)] * 6 + [spec(VMEM)],
        out_specs=spec(VMEM),
        scratch_shapes=[VMEM((LAYERS * 8, 128), F32)],
        compiler_params=PARAMS,
        cost_estimate=pl.CostEstimate(flops=20_000_000, bytes_accessed=4_000_000, transcendentals=0),
        name="inside",
    )(near, *constants, state)


def add_ghosts(last, near, diffusivity, part, sent, received):
    out_shape = struct(ROWS, 128) if last else [struct(ROWS, 128)] + PLANES
    out_specs = spec(pl.ANY) if last else [spec(VMEM)] * 5
    scratch = [VMEM((COMPS * SLOTS * BZ, 128), F32)] * 2
    if last:
        scratch += [VMEM((ROWS, 128), F32), pltpu.SemaphoreType.DMA((COMPS,))]
    return pl.pallas_call(
        functools.partial(ghost_kernel, last),
        out_shape=out_shape,
        in_specs=[spec(SMEM)] * 2 + [spec(VMEM)] * 9,
        out_specs=out_specs,
        scratch_shapes=scratch,
        compiler_params=PARAMS,
        name="ghosts_last" if last else "ghosts",
    )(near, diffusivity, part, *sent, *received)


def shards(
    old_state,
    new_owner,
    new_slot,
    neighbours,
    diffusivity,
    stoichiometry,
    heat_release,
    prefactor,
    activation,
):
    count_x = lax.axis_size("gx")
    count_y = lax.axis_size("gy")
    target = new_owner * SLOTS + new_slot
    old_rows = old_state.reshape(SLOTS, COMPS, 128, 128).transpose(1, 2, 0, 3).reshape(ROWS, 128)
    boxes, outbox_x, outbox_y = pl.pallas_call(
        functools.partial(pack_kernel, count_y),
        out_shape=[struct(ROWS, 128), struct(BZ, PIECE, 128), struct(1, YBOX, 128)],
        in_specs=[spec(SMEM), spec(VMEM)],
        out_specs=[spec(VMEM)] * 3,
        compiler_params=PARAMS,
        name="pack",
    )(target, old_rows)
    all_y = lax.all_gather(outbox_y, "gy", axis=0, tiled=True)
    pieces = lax.all_to_all(outbox_x, "gx", 0, 0, tiled=True)
    first, second, more = pl.pallas_call(
        sort_kernel,
        out_shape=[struct(count_x, PIECE, 128)] * 2 + [struct(1, dtype=jnp.int32)],
        in_specs=[spec(VMEM)],
        out_specs=[spec(VMEM)] * 2 + [spec(SMEM)],
        scratch_shapes=[SMEM((count_x,), jnp.int32)],
        compiler_params=PARAMS,
        name="sort",
    )(pieces)
    first = lax.all_to_all(first, "gx", 0, 0, tiled=True)
    second = lax.cond(
        more[0] > 0,
        lambda value: lax.all_to_all(value, "gx", 0, 0, tiled=True),
        lambda value: value,
        second,
    )
    state = pl.pallas_call(
        functools.partial(place_kernel, count_y),
        out_shape=struct(ROWS, 128),
        in_specs=[spec(SMEM)] + [spec(VMEM)] * 3,
        out_specs=spec(VMEM),
        compiler_params=PARAMS,
        name="place",
    )(target, boxes, first, second)
    state, *planes = pl.pallas_call(
        place_y_kernel,
        out_shape=[struct(ROWS, 128)] + PLANES,
        in_specs=[spec(VMEM), spec(pl.ANY)],
        out_specs=[spec(VMEM)] * 5,
        input_output_aliases={0: 0},
        scratch_shapes=[
            VMEM((count_y, TAG, 128), F32),
            pltpu.SemaphoreType.DMA,
            pltpu.SemaphoreType.DMA((SLOTS,)),
        ],
        compiler_params=PARAMS,
        name="place_y",
    )(state, all_y)
    constants = (diffusivity, stoichiometry, heat_release, prefactor, activation)
    for step_index in range(STEPS):
        x_a, x_b, y_a, y_b = planes
        received = (swapped(x_a, "gx", 0), swapped(x_b, "gx", 1), swapped(y_a, "gy", 0), swapped(y_b, "gy", 1))
        part = inside(neighbours, constants, state)
        if step_index < STEPS - 1:
            state, *planes = add_ghosts(False, neighbours, diffusivity, part, planes, received)
        else:
            state = add_ghosts(True, neighbours, diffusivity, part, planes, received)
    return state.reshape(COMPS, 128, SLOTS, 128).transpose(2, 0, 1, 3).reshape(SLOTS, COMPS, BZ * BX * BX)


def solution(mesh):
    return jax.shard_map(
        shards,
        mesh=mesh,
        in_specs=(
            P(("gx", "gy"), None, None),
            P(("gx", "gy")),
            P(("gx", "gy")),
            P(("gx", "gy"), None),
            P(),
            P(),
            P(),
            P(),
            P(),
        ),
        out_specs=P(("gx", "gy"), None, None),
        check_vma=False,
    )
```

```python
import functools

import jax
import jax.numpy as jnp
from jax import lax
from jax.experimental import pallas as pl
from jax.experimental.pallas import tpu as pltpu
from jax.sharding import PartitionSpec as P

NSPEC = 9
COMPS = 13
TEMP = 12
BX = 32
BZ = 16
SLOTS = 2
STEPS = 3
LAYERS = SLOTS * BZ
LROWS = COMPS * 8
BROWS = BZ * LROWS
ROWS = SLOTS * BROWS
TAG = 8
PIECE = LROWS + TAG
YBOX = BROWS + TAG
NONE = -1.0
SMEM = pltpu.SMEM
VMEM = pltpu.VMEM
F32 = jnp.float32
PARAMS = pltpu.CompilerParams(vmem_limit_bytes=48 * 1024 * 1024)


def swapped(value, axis, first):
    count = lax.axis_size(axis)
    pairs = []
    for low in range(first, count + first, 2):
        pairs += [(low % count, (low + 1) % count), ((low + 1) % count, low % count)]
    return lax.ppermute(value, axis, pairs)


def moves(target_ref, row, count_y, index_x, index_y):
    slot = lax.rem(target_ref[row], SLOTS)
    owner = target_ref[row] // SLOTS
    dest_x = owner // count_y
    dest_y = owner - dest_x * count_y
    goes_x = (dest_y == index_y) & (dest_x != index_x)
    goes_y = (dest_x == index_x) & (dest_y != index_y)
    return dest_x, dest_y, slot, goes_x, goes_y


def source_rows(n, z, c):
    return pl.ds(c * 256 + z * 16 + n, 8, stride=2)


def pack_kernel(count_y, target_ref, old_ref, box_ref, outx_ref, outy_ref):
    index_x = lax.axis_index("gx")
    index_y = lax.axis_index("gy")
    row_x = jnp.int32(0)
    row_y = jnp.int32(0)
    tag_x = jnp.int32(-1)
    tag_y = jnp.int32(-1)
    for n in range(SLOTS):
        dest_x, dest_y, slot, goes_x, goes_y = moves(target_ref, n, count_y, index_x, index_y)
        row_x = jnp.where(goes_x, n, row_x)
        row_y = jnp.where(goes_y, n, row_y)
        tag_x = jnp.where(goes_x, dest_x * SLOTS + slot, tag_x)
        tag_y = jnp.where(goes_y, dest_y * SLOTS + slot, tag_y)
    first_x = jnp.full((8, 128), row_x, jnp.int32) == 0
    first_y = jnp.full((8, 128), row_y, jnp.int32) == 0

    def layer(z, carry):
        row = pl.multiple_of(z * LROWS, 8)
        for c in range(COMPS):
            zero = old_ref[source_rows(0, z, c), :]
            one = old_ref[source_rows(1, z, c), :]
            box_ref[pl.ds(row + c * 8, 8), :] = zero
            box_ref[pl.ds(BROWS + row + c * 8, 8), :] = one
            outx_ref[z, c * 8 : c * 8 + 8, :] = jnp.where(first_x, zero, one)
            outy_ref[0, pl.ds(row + c * 8, 8), :] = jnp.where(first_y, zero, one)
        outx_ref[z, LROWS:, :] = jnp.full((TAG, 128), tag_x, jnp.int32).astype(F32)
        return carry

    lax.fori_loop(0, BZ, layer, 0)
    outy_ref[0, BROWS:, :] = jnp.full((TAG, 128), tag_y, jnp.int32).astype(F32)


def tag_of(tile):
    return jnp.max(tile).astype(jnp.int32)


def sort_kernel(pieces_ref, first_ref, second_ref, more_ref, used_ref):
    count = pieces_ref.shape[0]
    empty = jnp.full((TAG, 128), NONE, F32)
    more_ref[0] = 0
    tags = []
    for d in range(count):
        first_ref[d, LROWS:, :] = empty
        second_ref[d, LROWS:, :] = empty
        used_ref[d] = 0
        tags.append(tag_of(pieces_ref[d, LROWS:, :]))
    for s in range(count):
        tag = tags[s]
        there = jnp.maximum(tag, 0) // SLOTS
        used = used_ref[there]

        @pl.when((tag >= 0) & (used == 0))
        def _():
            first_ref[there, :, :] = pieces_ref[s]
            used_ref[there] = 1

        @pl.when((tag >= 0) & (used == 1))
        def _():
            second_ref[there, :, :] = pieces_ref[s]
            more_ref[0] = 1


def roll(value, shift, axis):
    if isinstance(shift, int):
        shift = shift % value.shape[axis]
        if shift == 0:
            return value
        return pltpu.roll(value, shift, axis)
    return pltpu.roll(value, lax.rem(shift + 256, 128), axis)


def lanes():
    return lax.broadcasted_iota(jnp.int32, (8, 128), 1)


def sublanes():
    return lax.broadcasted_iota(jnp.int32, (8, 128), 0)


def tile(row):
    return pl.ds(pl.multiple_of(row, 8), 8)


def put_faces(value_of, state_ref, out_refs):
    lane = lanes()
    ends = ((lane & 31) == 0) | ((lane & 31) == 31)
    even = (lane & 1) == 0
    group = lane >> 5
    even_x = lax.rem(lax.axis_index("gx"), 2) == 0
    even_y = lax.rem(lax.axis_index("gy"), 2) == 0
    xa_ref, xb_ref, ya_ref, yb_ref = out_refs

    for c in range(COMPS):
        rows = pl.ds(c * 8, 8)
        both = []
        for n in range(SLOTS):
            parts = [roll(jnp.where(ends, value_of(n, z, c), 0.0), 2 * z, 1) for z in range(BZ)]
            while len(parts) > 1:
                parts = [a + b for a, b in zip(parts[::2], parts[1::2])]
            both.append(parts[0])
        other = roll(both[1], 1, 1)
        low = jnp.where(even, both[0], other)
        high = jnp.where(even, other, both[0])
        xa_ref[rows, :] = jnp.where(even_x, high, low)
        xb_ref[rows, :] = jnp.where(even_x, low, high)
        low = jnp.zeros((8, 128), F32)
        high = jnp.zeros((8, 128), F32)
        for n in range(SLOTS):
            for half in range(2):
                where = 2 * n + half
                base = n * BROWS + half * 8 * LROWS + c * 8
                bottom = state_ref[pl.ds(base, 8, stride=LROWS), :]
                top = state_ref[pl.ds(base + 7, 8, stride=LROWS), :]
                low = jnp.where(group == where, roll(bottom, 32 * where, 1), low)
                high = jnp.where(group == where, roll(top, 32 * where - 96, 1), high)
        ya_ref[rows, :] = jnp.where(even_y, high, low)
        yb_ref[rows, :] = jnp.where(even_y, low, high)


STOI = COMPS
HEAT = STOI + NSPEC
PRE = HEAT + 1
ACT = PRE + 1
NEAR = ACT + 1
TABLES = (NEAR + 6 * SLOTS) * 8


def entry(table_ref, k):
    return table_ref[k * 8 : k * 8 + 8, :]


def place_kernel(
    count_y, target_ref, near_ref, diff_ref, stoi_ref, heat_ref, pre_ref, act_ref,
    box_ref, first_ref, second_ref, state_ref, table_ref,
):
    constants = [diff_ref[c] for c in range(COMPS)] + [stoi_ref[c] for c in range(NSPEC)]
    constants += [heat_ref[0], pre_ref[0], act_ref[0]]
    for k, constant in enumerate(constants):
        table_ref[k * 8 : k * 8 + 8, :] = jnp.full((8, 128), constant, F32)
    for side in range(6):
        for n in range(SLOTS):
            k = NEAR + side * SLOTS + n
            table_ref[k * 8 : k * 8 + 8, :] = jnp.full((8, 128), near_ref[n, side], jnp.int32).astype(F32)
    index_x = lax.axis_index("gx")
    index_y = lax.axis_index("gy")
    tags = [tag_of(source[0, LROWS:, :]) for source in (first_ref, second_ref)]

    def put(slot, z, value):
        state_ref[pl.ds(pl.multiple_of(slot * BROWS + z * LROWS, 8), LROWS), :] = value

    for n in range(SLOTS):
        dest_x, dest_y, slot, goes_x, goes_y = moves(target_ref, n, count_y, index_x, index_y)

        @pl.when((dest_x == index_x) & (dest_y == index_y))
        def _():
            for z in range(BZ):
                put(slot, z, box_ref[pl.ds(n * BROWS + z * LROWS, LROWS), :])

    for tag, source in zip(tags, (first_ref, second_ref)):

        @pl.when(tag >= 0)
        def _():
            for z in range(BZ):
                put(lax.rem(tag, SLOTS), z, source[z, :LROWS, :])


def place_y_kernel(_, ally_ref, state_ref, xa_ref, xb_ref, ya_ref, yb_ref, tag_ref, tag_sem, sems):
    load = pltpu.make_async_copy(ally_ref.at[:, pl.ds(BROWS, TAG), :], tag_ref, tag_sem)
    load.start()
    index_y = jnp.full((TAG, 128), lax.axis_index("gy"), jnp.int32)
    load.wait()
    places = []
    for slot in range(SLOTS):
        wanted = (index_y * SLOTS + slot).astype(F32)
        hits = [jnp.where(tag_ref[p] == wanted, p + 1.0, 0.0) for p in range(tag_ref.shape[0])]
        places.append(tag_of(functools.reduce(jnp.maximum, hits)))
    boxes = [
        pltpu.make_async_copy(
            ally_ref.at[jnp.maximum(place - 1, 0), pl.ds(0, BROWS), :],
            state_ref.at[pl.ds(slot * BROWS, BROWS), :],
            sems.at[slot],
        )
        for slot, place in enumerate(places)
    ]
    for place, box in zip(places, boxes):

        @pl.when(place > 0)
        def _():
            box.start()

    for place, box in zip(places, boxes):

        @pl.when(place > 0)
        def _():
            box.wait()

    put_faces(
        lambda n, z, c: state_ref[pl.ds((n * BZ + z) * LROWS + c * 8, 8), :],
        state_ref,
        (xa_ref, xb_ref, ya_ref, yb_ref),
    )


def power(value):
    return jnp.exp(0.7 * jnp.log(value))


UNROLL = 8


def inside_kernel(table_ref, state_ref, new_ref, coef_ref):
    lane = lanes()
    sub = sublanes()
    y_low_lanes = lane < 32
    y_high_lanes = lane >= 96
    inner = [
        (lane & 31) != 0,
        (lane & 31) != 31,
        ~(y_low_lanes & (sub == 0)),
        ~(y_high_lanes & (sub == 7)),
    ]

    def power_layer(block, carry):
        for u in range(8):
            index = block * 8 + u
            coef_ref[tile(index * 8), :] = power(state_ref[tile(index * LROWS + TEMP * 8), :])
        return carry

    lax.fori_loop(0, LAYERS // 8, power_layer, 0)

    def layer(n, z, z_unrolled):
        index = n * BZ + z
        first = jnp.full((8, 128), z, jnp.int32) == 0
        last = jnp.full((8, 128), z, jnp.int32) == BZ - 1
        index_m = jnp.maximum(index - 1, 0)
        index_p = jnp.minimum(index + 1, LAYERS - 1)
        near_m = table_ref[tile((NEAR + 4 * SLOTS + n) * 8), :]
        near_p = table_ref[tile((NEAR + 5 * SLOTS + n) * 8), :]

        def layers_beside(load):
            below, above = load(index_m), load(index_p)
            if z_unrolled == 0:
                ghost = jnp.where(near_m < 0, load(index), jnp.where(near_m == 0, load(BZ - 1), load(2 * BZ - 1)))
                below = jnp.where(first, ghost, below)
            if z_unrolled == UNROLL - 1:
                ghost = jnp.where(near_p < 0, load(index), jnp.where(near_p == 0, load(0), load(BZ)))
                above = jnp.where(last, ghost, above)
            return below, above

        def beside(value):
            down = roll(value, 32, 1)
            up = roll(value, -32, 1)
            return (
                roll(value, 1, 1),
                roll(value, -1, 1),
                jnp.where(y_low_lanes, roll(down, 1, 0), down),
                jnp.where(y_high_lanes, roll(up, -1, 0), up),
            )

        center = coef_ref[tile(index * 8), :]
        weights = [
            jnp.where(mask, 0.5 * (center + side), 0.0) for mask, side in zip(inner, beside(center))
        ]
        for side in layers_beside(lambda at: coef_ref[tile(at * 8), :]):
            weights.append(0.5 * (center + side))
        total = functools.reduce(lambda a, b: a + b, weights)
        row = pl.multiple_of(index * LROWS, 8)
        rate = (
            entry(table_ref, PRE)
            * state_ref[pl.ds(row, 8), :]
            * state_ref[pl.ds(row + 8, 8), :]
            * jnp.exp(-entry(table_ref, ACT) / state_ref[pl.ds(row + TEMP * 8, 8), :])
        )
        for c in range(COMPS):
            value = state_ref[pl.ds(row + c * 8, 8), :]
            sides = beside(value)
            sides = sides + layers_beside(lambda at: state_ref[tile(at * LROWS + c * 8), :])
            change = -total * value
            for weight, side in zip(weights, sides):
                change = change + weight * side
            value = value + entry(table_ref, c) * change
            if c < NSPEC:
                value = value + entry(table_ref, STOI + c) * rate
            elif c == TEMP:
                value = value + entry(table_ref, HEAT) * rate
            new_ref[pl.ds(row + c * 8, 8), :] = value

    def layers(block, carry):
        n = block // (BZ // UNROLL)
        z = (block - n * (BZ // UNROLL)) * UNROLL
        for u in range(UNROLL):
            layer(n, z + u, u)
        return carry

    lax.fori_loop(0, LAYERS // UNROLL, layers, 0)


def ghost_kernel(last, table_ref, part_ref, *refs):
    own_refs, got_refs = refs[:4], refs[4:8]
    if last:
        out_ref, ym_ref, yp_ref, new_ref, sems = refs[8:]
    else:
        new_ref, *out_refs, ym_ref, yp_ref = refs[8:]
    lane = lanes()
    even = (lane & 1) == 0
    ends = ((lane & 31) == 0) | ((lane & 31) == 31)
    first_box = lane < 64
    y_first = (lane < 32) & (sublanes() == 0)
    y_last = (lane >= 96) & (sublanes() == 7)
    even_x = lax.rem(lax.axis_index("gx"), 2) == 0
    even_y = lax.rem(lax.axis_index("gy"), 2) == 0

    def first_slot(n, side):
        return entry(table_ref, NEAR + side * SLOTS + n) == 0

    def plane_pairs(c):
        rows = slice(c * 8, c * 8 + 8)
        own_a, own_b, own_ya, own_yb = (ref[rows, :] for ref in own_refs)
        got_a, got_b, got_ya, got_yb = (ref[rows, :] for ref in got_refs)
        low = jnp.where(even_x, own_b, own_a)
        high = jnp.where(even_x, own_a, own_b)
        below = jnp.where(even_x, got_b, got_a)
        above = jnp.where(even_x, got_a, got_b)
        own = (jnp.where(even, low, high), roll(jnp.where(even, high, low), -1, 1))
        pairs = []
        below = (roll(below, -31, 1), roll(below, -32, 1))
        above = (roll(above, 31, 1), roll(above, 30, 1))
        for n in range(SLOTS):
            ghost = jnp.where(
                even, jnp.where(first_slot(n, 0), *below), jnp.where(first_slot(n, 1), *above)
            )
            pairs.append((own[n], ghost))
        low = jnp.where(even_y, own_yb, own_ya)
        high = jnp.where(even_y, own_ya, own_yb)
        below = jnp.where(even_y, got_yb, got_ya)
        above = jnp.where(even_y, got_ya, got_yb)
        for side, mine, theirs in ((2, low, below), (3, high, above)):
            other = roll(theirs, 64, 1)
            ghost = jnp.where(
                first_box,
                jnp.where(first_slot(0, side), theirs, other),
                jnp.where(first_slot(1, side), other, theirs),
            )
            pairs.append((mine, ghost))
        return pairs

    weights = [0.5 * (power(own) + power(ghost)) for own, ghost in plane_pairs(TEMP)]
    x_terms = []
    for c in range(COMPS):
        terms = [
            entry(table_ref, c) * (weight * (ghost - own)) for weight, (own, ghost) in zip(weights, plane_pairs(c))
        ]
        x_terms.append(terms[:SLOTS])
        for n in range(SLOTS):
            for half in range(2):
                where = 32 * (2 * n + half)
                rows = pl.ds((c * SLOTS + n) * BZ + half * 8, 8)
                ym_ref[rows, :] = roll(terms[2], -where, 1)
                yp_ref[rows, :] = roll(terms[3], 96 - where, 1)

    def value_of(n, z, c):
        row = (n * BZ + z) * LROWS + c * 8
        at = pl.ds((c * SLOTS + n) * BZ + z, 1)
        value = part_ref[pl.ds(row, 8), :] + jnp.where(ends, roll(x_terms[c][n], -2 * z, 1), 0.0)
        low = jnp.broadcast_to(ym_ref[at, :], (8, 128))
        high = jnp.broadcast_to(yp_ref[at, :], (8, 128))
        value = value + jnp.where(y_first, low, jnp.where(y_last, high, 0.0))
        if last:
            new_ref[source_rows(n, z, c), :] = value
        else:
            new_ref[pl.ds(row, 8), :] = value
        return value

    if last:
        stores = []
        for c in range(COMPS):
            for n in range(SLOTS):
                for z in range(BZ):
                    value_of(n, z, c)
            rows = pl.ds(c * 256, 256)
            stores.append(pltpu.make_async_copy(new_ref.at[rows, :], out_ref.at[rows, :], sems.at[c]))
            stores[c].start()
        for store in stores:
            store.wait()
    else:
        put_faces(value_of, new_ref, out_refs)


def spec(space):
    return pl.BlockSpec(memory_space=space)


def struct(*shape, dtype=F32):
    return jax.ShapeDtypeStruct(shape, dtype)


PLANES = [struct(LROWS, 128)] * 4


def inside(table, state):
    return pl.pallas_call(
        inside_kernel,
        out_shape=struct(ROWS, 128),
        in_specs=[spec(VMEM)] * 2,
        out_specs=spec(VMEM),
        scratch_shapes=[VMEM((LAYERS * 8, 128), F32)],
        compiler_params=PARAMS,
        cost_estimate=pl.CostEstimate(flops=20_000_000, bytes_accessed=4_000_000, transcendentals=0),
        name="inside",
    )(table, state)


def add_ghosts(last, table, part, sent, received):
    out_shape = struct(ROWS, 128) if last else [struct(ROWS, 128)] + PLANES
    out_specs = spec(pl.ANY) if last else [spec(VMEM)] * 5
    scratch = [VMEM((COMPS * SLOTS * BZ, 128), F32)] * 2
    if last:
        scratch += [VMEM((ROWS, 128), F32), pltpu.SemaphoreType.DMA((COMPS,))]
    return pl.pallas_call(
        functools.partial(ghost_kernel, last),
        out_shape=out_shape,
        in_specs=[spec(VMEM)] * 10,
        out_specs=out_specs,
        scratch_shapes=scratch,
        compiler_params=PARAMS,
        name="ghosts_last" if last else "ghosts",
    )(table, part, *sent, *received)


def shards(
    old_state,
    new_owner,
    new_slot,
    neighbours,
    diffusivity,
    stoichiometry,
    heat_release,
    prefactor,
    activation,
):
    count_x = lax.axis_size("gx")
    count_y = lax.axis_size("gy")
    target = new_owner * SLOTS + new_slot
    old_rows = old_state.reshape(SLOTS, COMPS, 128, 128).transpose(1, 2, 0, 3).reshape(ROWS, 128)
    boxes, outbox_x, outbox_y = pl.pallas_call(
        functools.partial(pack_kernel, count_y),
        out_shape=[struct(ROWS, 128), struct(BZ, PIECE, 128), struct(1, YBOX, 128)],
        in_specs=[spec(SMEM), spec(VMEM)],
        out_specs=[spec(VMEM)] * 3,
        compiler_params=PARAMS,
        name="pack",
    )(target, old_rows)
    all_y = lax.all_gather(outbox_y, "gy", axis=0, tiled=True)
    pieces = lax.all_to_all(outbox_x, "gx", 0, 0, tiled=True)
    first, second, more = pl.pallas_call(
        sort_kernel,
        out_shape=[struct(count_x, PIECE, 128)] * 2 + [struct(1, dtype=jnp.int32)],
        in_specs=[spec(VMEM)],
        out_specs=[spec(VMEM)] * 2 + [spec(SMEM)],
        scratch_shapes=[SMEM((count_x,), jnp.int32)],
        compiler_params=PARAMS,
        name="sort",
    )(pieces)
    first = lax.all_to_all(first, "gx", 0, 0, tiled=True)
    second = lax.cond(
        more[0] > 0,
        lambda value: lax.all_to_all(value, "gx", 0, 0, tiled=True),
        lambda value: value,
        second,
    )
    constants = (diffusivity, stoichiometry, heat_release, prefactor, activation)
    state, table = pl.pallas_call(
        functools.partial(place_kernel, count_y),
        out_shape=[struct(ROWS, 128), struct(TABLES, 128)],
        in_specs=[spec(SMEM)] * 7 + [spec(VMEM)] * 3,
        out_specs=[spec(VMEM)] * 2,
        compiler_params=PARAMS,
        name="place",
    )(target, neighbours, *constants, boxes, first, second)
    state, *planes = pl.pallas_call(
        place_y_kernel,
        out_shape=[struct(ROWS, 128)] + PLANES,
        in_specs=[spec(VMEM), spec(pl.ANY)],
        out_specs=[spec(VMEM)] * 5,
        input_output_aliases={0: 0},
        scratch_shapes=[
            VMEM((count_y, TAG, 128), F32),
            pltpu.SemaphoreType.DMA,
            pltpu.SemaphoreType.DMA((SLOTS,)),
        ],
        compiler_params=PARAMS,
        name="place_y",
    )(state, all_y)
    for step_index in range(STEPS):
        x_a, x_b, y_a, y_b = planes
        received = (swapped(x_a, "gx", 0), swapped(x_b, "gx", 1), swapped(y_a, "gy", 0), swapped(y_b, "gy", 1))
        part = inside(table, state)
        if step_index < STEPS - 1:
            state, *planes = add_ghosts(False, table, part, planes, received)
        else:
            state = add_ghosts(True, table, part, planes, received)
    return state.reshape(COMPS, 128, SLOTS, 128).transpose(2, 0, 1, 3).reshape(SLOTS, COMPS, BZ * BX * BX)


def solution(mesh):
    return jax.shard_map(
        shards,
        mesh=mesh,
        in_specs=(
            P(("gx", "gy"), None, None),
            P(("gx", "gy")),
            P(("gx", "gy")),
            P(("gx", "gy"), None),
            P(),
            P(),
            P(),
            P(),
            P(),
        ),
        out_specs=P(("gx", "gy"), None, None),
        check_vma=False,
    )
```

```python
import functools

import jax
import jax.numpy as jnp
from jax import lax
from jax.experimental import pallas as pl
from jax.experimental.pallas import tpu as pltpu
from jax.sharding import PartitionSpec as P

NSPEC = 9
COMPS = 13
TEMP = 12
BX = 32
BZ = 16
SLOTS = 2
STEPS = 3
LAYERS = SLOTS * BZ
LROWS = COMPS * 8
BROWS = BZ * LROWS
ROWS = SLOTS * BROWS
TAG = 8
PIECE = LROWS + TAG
YBOX = BROWS + TAG
NONE = -1.0
SMEM = pltpu.SMEM
VMEM = pltpu.VMEM
F32 = jnp.float32
PARAMS = pltpu.CompilerParams(vmem_limit_bytes=16 * 1024 * 1024)


def swapped(value, axis, first):
    count = lax.axis_size(axis)
    pairs = []
    for low in range(first, count + first, 2):
        pairs += [(low % count, (low + 1) % count), ((low + 1) % count, low % count)]
    return lax.ppermute(value, axis, pairs)


def moves(target_ref, row, count_y, index_x, index_y):
    slot = lax.rem(target_ref[row], SLOTS)
    owner = target_ref[row] // SLOTS
    dest_x = owner // count_y
    dest_y = owner - dest_x * count_y
    goes_x = (dest_y == index_y) & (dest_x != index_x)
    goes_y = (dest_x == index_x) & (dest_y != index_y)
    return dest_x, dest_y, slot, goes_x, goes_y


def source_rows(n, z, c):
    return pl.ds(c * 256 + z * 16 + n, 8, stride=2)


def pack_kernel(count_y, target_ref, old_ref, box_ref, outx_ref, outy_ref):
    index_x = lax.axis_index("gx")
    index_y = lax.axis_index("gy")
    row_x = jnp.int32(0)
    row_y = jnp.int32(0)
    tag_x = jnp.int32(-1)
    tag_y = jnp.int32(-1)
    for n in range(SLOTS):
        dest_x, dest_y, slot, goes_x, goes_y = moves(target_ref, n, count_y, index_x, index_y)
        row_x = jnp.where(goes_x, n, row_x)
        row_y = jnp.where(goes_y, n, row_y)
        tag_x = jnp.where(goes_x, dest_x * SLOTS + slot, tag_x)
        tag_y = jnp.where(goes_y, dest_y * SLOTS + slot, tag_y)
    first_x = jnp.full((8, 128), row_x, jnp.int32) == 0
    first_y = jnp.full((8, 128), row_y, jnp.int32) == 0

    def layer(z, carry):
        row = pl.multiple_of(z * LROWS, 8)
        for c in range(COMPS):
            zero = old_ref[source_rows(0, z, c), :]
            one = old_ref[source_rows(1, z, c), :]
            box_ref[pl.ds(row + c * 8, 8), :] = zero
            box_ref[pl.ds(BROWS + row + c * 8, 8), :] = one
            outx_ref[z, c * 8 : c * 8 + 8, :] = jnp.where(first_x, zero, one)
            outy_ref[0, pl.ds(row + c * 8, 8), :] = jnp.where(first_y, zero, one)
        outx_ref[z, LROWS:, :] = jnp.full((TAG, 128), tag_x, jnp.int32).astype(F32)
        return carry

    lax.fori_loop(0, BZ, layer, 0)
    outy_ref[0, BROWS:, :] = jnp.full((TAG, 128), tag_y, jnp.int32).astype(F32)


def tag_of(tile):
    return jnp.max(tile).astype(jnp.int32)


def sort_kernel(pieces_ref, first_ref, second_ref, more_ref, used_ref):
    count = pieces_ref.shape[0]
    empty = jnp.full((TAG, 128), NONE, F32)
    more_ref[0] = 0
    tags = []
    for d in range(count):
        first_ref[d, LROWS:, :] = empty
        second_ref[d, LROWS:, :] = empty
        used_ref[d] = 0
        tags.append(tag_of(pieces_ref[d, LROWS:, :]))
    for s in range(count):
        tag = tags[s]
        there = jnp.maximum(tag, 0) // SLOTS
        used = used_ref[there]

        @pl.when((tag >= 0) & (used == 0))
        def _():
            first_ref[there, :, :] = pieces_ref[s]
            used_ref[there] = 1

        @pl.when((tag >= 0) & (used == 1))
        def _():
            second_ref[there, :, :] = pieces_ref[s]
            more_ref[0] = 1


def roll(value, shift, axis):
    if isinstance(shift, int):
        shift = shift % value.shape[axis]
        if shift == 0:
            return value
        return pltpu.roll(value, shift, axis)
    return pltpu.roll(value, lax.rem(shift + 256, 128), axis)


def lanes():
    return lax.broadcasted_iota(jnp.int32, (8, 128), 1)


def sublanes():
    return lax.broadcasted_iota(jnp.int32, (8, 128), 0)


def tile(row):
    return pl.ds(pl.multiple_of(row, 8), 8)


def put_faces(value_of, state_ref, out_refs):
    lane = lanes()
    ends = ((lane & 31) == 0) | ((lane & 31) == 31)
    even = (lane & 1) == 0
    group = lane >> 5
    even_x = lax.rem(lax.axis_index("gx"), 2) == 0
    even_y = lax.rem(lax.axis_index("gy"), 2) == 0
    xa_ref, xb_ref, ya_ref, yb_ref = out_refs

    for c in range(COMPS):
        rows = pl.ds(c * 8, 8)
        both = []
        for n in range(SLOTS):
            parts = [roll(jnp.where(ends, value_of(n, z, c), 0.0), 2 * z, 1) for z in range(BZ)]
            while len(parts) > 1:
                parts = [a + b for a, b in zip(parts[::2], parts[1::2])]
            both.append(parts[0])
        other = roll(both[1], 1, 1)
        low = jnp.where(even, both[0], other)
        high = jnp.where(even, other, both[0])
        xa_ref[rows, :] = jnp.where(even_x, high, low)
        xb_ref[rows, :] = jnp.where(even_x, low, high)
        low = jnp.zeros((8, 128), F32)
        high = jnp.zeros((8, 128), F32)
        for n in range(SLOTS):
            for half in range(2):
                where = 2 * n + half
                base = n * BROWS + half * 8 * LROWS + c * 8
                bottom = state_ref[pl.ds(base, 8, stride=LROWS), :]
                top = state_ref[pl.ds(base + 7, 8, stride=LROWS), :]
                low = jnp.where(group == where, roll(bottom, 32 * where, 1), low)
                high = jnp.where(group == where, roll(top, 32 * where - 96, 1), high)
        ya_ref[rows, :] = jnp.where(even_y, high, low)
        yb_ref[rows, :] = jnp.where(even_y, low, high)


STOI = COMPS
HEAT = STOI + NSPEC
PRE = HEAT + 1
ACT = PRE + 1
NEAR = ACT + 1
TABLES = (NEAR + 6 * SLOTS) * 8


def entry(table_ref, k):
    return table_ref[k * 8 : k * 8 + 8, :]


def place_kernel(
    count_y, target_ref, near_ref, diff_ref, stoi_ref, heat_ref, pre_ref, act_ref,
    box_ref, first_ref, second_ref, state_ref, table_ref,
):
    constants = [diff_ref[c] for c in range(COMPS)] + [stoi_ref[c] for c in range(NSPEC)]
    constants += [heat_ref[0], pre_ref[0], act_ref[0]]
    for k, constant in enumerate(constants):
        table_ref[k * 8 : k * 8 + 8, :] = jnp.full((8, 128), constant, F32)
    for side in range(6):
        for n in range(SLOTS):
            k = NEAR + side * SLOTS + n
            table_ref[k * 8 : k * 8 + 8, :] = jnp.full((8, 128), near_ref[n, side], jnp.int32).astype(F32)
    index_x = lax.axis_index("gx")
    index_y = lax.axis_index("gy")
    tags = [tag_of(source[0, LROWS:, :]) for source in (first_ref, second_ref)]

    def put(slot, z, value):
        state_ref[pl.ds(pl.multiple_of(slot * BROWS + z * LROWS, 8), LROWS), :] = value

    for n in range(SLOTS):
        dest_x, dest_y, slot, goes_x, goes_y = moves(target_ref, n, count_y, index_x, index_y)

        @pl.when((dest_x == index_x) & (dest_y == index_y))
        def _():
            for z in range(BZ):
                put(slot, z, box_ref[pl.ds(n * BROWS + z * LROWS, LROWS), :])

    for tag, source in zip(tags, (first_ref, second_ref)):

        @pl.when(tag >= 0)
        def _():
            for z in range(BZ):
                put(lax.rem(tag, SLOTS), z, source[z, :LROWS, :])


def place_y_kernel(_, ally_ref, state_ref, xa_ref, xb_ref, ya_ref, yb_ref, tag_ref, tag_sem, sems):
    load = pltpu.make_async_copy(ally_ref.at[:, pl.ds(BROWS, TAG), :], tag_ref, tag_sem)
    load.start()
    index_y = jnp.full((TAG, 128), lax.axis_index("gy"), jnp.int32)
    load.wait()
    places = []
    for slot in range(SLOTS):
        wanted = (index_y * SLOTS + slot).astype(F32)
        hits = [jnp.where(tag_ref[p] == wanted, p + 1.0, 0.0) for p in range(tag_ref.shape[0])]
        places.append(tag_of(functools.reduce(jnp.maximum, hits)))
    boxes = [
        pltpu.make_async_copy(
            ally_ref.at[jnp.maximum(place - 1, 0), pl.ds(0, BROWS), :],
            state_ref.at[pl.ds(slot * BROWS, BROWS), :],
            sems.at[slot],
        )
        for slot, place in enumerate(places)
    ]
    for place, box in zip(places, boxes):

        @pl.when(place > 0)
        def _():
            box.start()

    for place, box in zip(places, boxes):

        @pl.when(place > 0)
        def _():
            box.wait()

    put_faces(
        lambda n, z, c: state_ref[pl.ds((n * BZ + z) * LROWS + c * 8, 8), :],
        state_ref,
        (xa_ref, xb_ref, ya_ref, yb_ref),
    )


def power(value):
    return jnp.exp(0.7 * jnp.log(value))


UNROLL = 8


def inside_kernel(table_ref, state_ref, new_ref, coef_ref):
    lane = lanes()
    sub = sublanes()
    y_low_lanes = lane < 32
    y_high_lanes = lane >= 96
    inner = [
        (lane & 31) != 0,
        (lane & 31) != 31,
        ~(y_low_lanes & (sub == 0)),
        ~(y_high_lanes & (sub == 7)),
    ]

    def power_layer(block, carry):
        for u in range(8):
            index = block * 8 + u
            coef_ref[tile(index * 8), :] = power(state_ref[tile(index * LROWS + TEMP * 8), :])
        return carry

    lax.fori_loop(0, LAYERS // 8, power_layer, 0)

    def layer(n, z, z_unrolled):
        index = n * BZ + z
        first = jnp.full((8, 128), z, jnp.int32) == 0
        last = jnp.full((8, 128), z, jnp.int32) == BZ - 1
        index_m = jnp.maximum(index - 1, 0)
        index_p = jnp.minimum(index + 1, LAYERS - 1)
        near_m = table_ref[tile((NEAR + 4 * SLOTS + n) * 8), :]
        near_p = table_ref[tile((NEAR + 5 * SLOTS + n) * 8), :]

        def layers_beside(load):
            below, above = load(index_m), load(index_p)
            if z_unrolled == 0:
                ghost = jnp.where(near_m < 0, load(index), jnp.where(near_m == 0, load(BZ - 1), load(2 * BZ - 1)))
                below = jnp.where(first, ghost, below)
            if z_unrolled == UNROLL - 1:
                ghost = jnp.where(near_p < 0, load(index), jnp.where(near_p == 0, load(0), load(BZ)))
                above = jnp.where(last, ghost, above)
            return below, above

        def beside(value):
            down = roll(value, 32, 1)
            up = roll(value, -32, 1)
            return (
                roll(value, 1, 1),
                roll(value, -1, 1),
                jnp.where(y_low_lanes, roll(down, 1, 0), down),
                jnp.where(y_high_lanes, roll(up, -1, 0), up),
            )

        center = coef_ref[tile(index * 8), :]
        weights = [
            jnp.where(mask, 0.5 * (center + side), 0.0) for mask, side in zip(inner, beside(center))
        ]
        for side in layers_beside(lambda at: coef_ref[tile(at * 8), :]):
            weights.append(0.5 * (center + side))
        total = functools.reduce(lambda a, b: a + b, weights)
        row = pl.multiple_of(index * LROWS, 8)
        rate = (
            entry(table_ref, PRE)
            * state_ref[pl.ds(row, 8), :]
            * state_ref[pl.ds(row + 8, 8), :]
            * jnp.exp(-entry(table_ref, ACT) / state_ref[pl.ds(row + TEMP * 8, 8), :])
        )
        for c in range(COMPS):
            value = state_ref[pl.ds(row + c * 8, 8), :]
            sides = beside(value)
            sides = sides + layers_beside(lambda at: state_ref[tile(at * LROWS + c * 8), :])
            change = -total * value
            for weight, side in zip(weights, sides):
                change = change + weight * side
            value = value + entry(table_ref, c) * change
            if c < NSPEC:
                value = value + entry(table_ref, STOI + c) * rate
            elif c == TEMP:
                value = value + entry(table_ref, HEAT) * rate
            new_ref[pl.ds(row + c * 8, 8), :] = value

    def layers(block, carry):
        n = block // (BZ // UNROLL)
        z = (block - n * (BZ // UNROLL)) * UNROLL
        for u in range(UNROLL):
            layer(n, z + u, u)
        return carry

    lax.fori_loop(0, LAYERS // UNROLL, layers, 0)


def ghost_kernel(last, table_ref, part_ref, *refs):
    own_refs, got_refs = refs[:4], refs[4:8]
    if last:
        out_ref, ym_ref, yp_ref, new_ref, sems = refs[8:]
    else:
        new_ref, *out_refs, ym_ref, yp_ref = refs[8:]
    lane = lanes()
    even = (lane & 1) == 0
    ends = ((lane & 31) == 0) | ((lane & 31) == 31)
    first_box = lane < 64
    y_first = (lane < 32) & (sublanes() == 0)
    y_last = (lane >= 96) & (sublanes() == 7)
    even_x = lax.rem(lax.axis_index("gx"), 2) == 0
    even_y = lax.rem(lax.axis_index("gy"), 2) == 0

    def first_slot(n, side):
        return entry(table_ref, NEAR + side * SLOTS + n) == 0

    def plane_pairs(c):
        rows = slice(c * 8, c * 8 + 8)
        own_a, own_b, own_ya, own_yb = (ref[rows, :] for ref in own_refs)
        got_a, got_b, got_ya, got_yb = (ref[rows, :] for ref in got_refs)
        low = jnp.where(even_x, own_b, own_a)
        high = jnp.where(even_x, own_a, own_b)
        below = jnp.where(even_x, got_b, got_a)
        above = jnp.where(even_x, got_a, got_b)
        own = (jnp.where(even, low, high), roll(jnp.where(even, high, low), -1, 1))
        pairs = []
        below = (roll(below, -31, 1), roll(below, -32, 1))
        above = (roll(above, 31, 1), roll(above, 30, 1))
        for n in range(SLOTS):
            ghost = jnp.where(
                even, jnp.where(first_slot(n, 0), *below), jnp.where(first_slot(n, 1), *above)
            )
            pairs.append((own[n], ghost))
        low = jnp.where(even_y, own_yb, own_ya)
        high = jnp.where(even_y, own_ya, own_yb)
        below = jnp.where(even_y, got_yb, got_ya)
        above = jnp.where(even_y, got_ya, got_yb)
        for side, mine, theirs in ((2, low, below), (3, high, above)):
            other = roll(theirs, 64, 1)
            ghost = jnp.where(
                first_box,
                jnp.where(first_slot(0, side), theirs, other),
                jnp.where(first_slot(1, side), other, theirs),
            )
            pairs.append((mine, ghost))
        return pairs

    weights = [0.5 * (power(own) + power(ghost)) for own, ghost in plane_pairs(TEMP)]
    x_terms = []
    for c in range(COMPS):
        terms = [
            entry(table_ref, c) * (weight * (ghost - own)) for weight, (own, ghost) in zip(weights, plane_pairs(c))
        ]
        x_terms.append(terms[:SLOTS])
        for n in range(SLOTS):
            for half in range(2):
                where = 32 * (2 * n + half)
                rows = pl.ds((c * SLOTS + n) * BZ + half * 8, 8)
                ym_ref[rows, :] = roll(terms[2], -where, 1)
                yp_ref[rows, :] = roll(terms[3], 96 - where, 1)

    def value_of(n, z, c):
        row = (n * BZ + z) * LROWS + c * 8
        at = pl.ds((c * SLOTS + n) * BZ + z, 1)
        value = part_ref[pl.ds(row, 8), :] + jnp.where(ends, roll(x_terms[c][n], -2 * z, 1), 0.0)
        low = jnp.broadcast_to(ym_ref[at, :], (8, 128))
        high = jnp.broadcast_to(yp_ref[at, :], (8, 128))
        value = value + jnp.where(y_first, low, jnp.where(y_last, high, 0.0))
        if last:
            new_ref[source_rows(n, z, c), :] = value
        else:
            new_ref[pl.ds(row, 8), :] = value
        return value

    if last:
        stores = []
        for c in range(COMPS):
            for n in range(SLOTS):
                for z in range(BZ):
                    value_of(n, z, c)
            rows = pl.ds(c * 256, 256)
            stores.append(pltpu.make_async_copy(new_ref.at[rows, :], out_ref.at[rows, :], sems.at[c]))
            stores[c].start()
        for store in stores:
            store.wait()
    else:
        put_faces(value_of, new_ref, out_refs)


def spec(space):
    return pl.BlockSpec(memory_space=space)


def struct(*shape, dtype=F32):
    return jax.ShapeDtypeStruct(shape, dtype)


PLANES = [struct(LROWS, 128)] * 4


def inside(table, state):
    return pl.pallas_call(
        inside_kernel,
        out_shape=struct(ROWS, 128),
        in_specs=[spec(VMEM)] * 2,
        out_specs=spec(VMEM),
        scratch_shapes=[VMEM((LAYERS * 8, 128), F32)],
        compiler_params=PARAMS,
        cost_estimate=pl.CostEstimate(flops=20_000_000, bytes_accessed=4_000_000, transcendentals=0),
        name="inside",
    )(table, state)


def add_ghosts(last, table, part, sent, received):
    out_shape = struct(ROWS, 128) if last else [struct(ROWS, 128)] + PLANES
    out_specs = spec(pl.ANY) if last else [spec(VMEM)] * 5
    scratch = [VMEM((COMPS * SLOTS * BZ, 128), F32)] * 2
    if last:
        scratch += [VMEM((ROWS, 128), F32), pltpu.SemaphoreType.DMA((COMPS,))]
    return pl.pallas_call(
        functools.partial(ghost_kernel, last),
        out_shape=out_shape,
        in_specs=[spec(VMEM)] * 10,
        out_specs=out_specs,
        scratch_shapes=scratch,
        compiler_params=PARAMS,
        name="ghosts_last" if last else "ghosts",
    )(table, part, *sent, *received)


def shards(
    old_state,
    new_owner,
    new_slot,
    neighbours,
    diffusivity,
    stoichiometry,
    heat_release,
    prefactor,
    activation,
):
    count_x = lax.axis_size("gx")
    count_y = lax.axis_size("gy")
    target = new_owner * SLOTS + new_slot
    old_rows = old_state.reshape(SLOTS, COMPS, 128, 128).transpose(1, 2, 0, 3).reshape(ROWS, 128)
    boxes, outbox_x, outbox_y = pl.pallas_call(
        functools.partial(pack_kernel, count_y),
        out_shape=[struct(ROWS, 128), struct(BZ, PIECE, 128), struct(1, YBOX, 128)],
        in_specs=[spec(SMEM), spec(VMEM)],
        out_specs=[spec(VMEM)] * 3,
        compiler_params=PARAMS,
        name="pack",
    )(target, old_rows)
    all_y = lax.all_gather(outbox_y, "gy", axis=0, tiled=True)
    pieces = lax.all_to_all(outbox_x, "gx", 0, 0, tiled=True)
    first, second, more = pl.pallas_call(
        sort_kernel,
        out_shape=[struct(count_x, PIECE, 128)] * 2 + [struct(1, dtype=jnp.int32)],
        in_specs=[spec(VMEM)],
        out_specs=[spec(VMEM)] * 2 + [spec(SMEM)],
        scratch_shapes=[SMEM((count_x,), jnp.int32)],
        compiler_params=PARAMS,
        name="sort",
    )(pieces)
    first = lax.all_to_all(first, "gx", 0, 0, tiled=True)
    second = lax.cond(
        more[0] > 0,
        lambda value: lax.all_to_all(value, "gx", 0, 0, tiled=True),
        lambda value: value,
        second,
    )
    constants = (diffusivity, stoichiometry, heat_release, prefactor, activation)
    state, table = pl.pallas_call(
        functools.partial(place_kernel, count_y),
        out_shape=[struct(ROWS, 128), struct(TABLES, 128)],
        in_specs=[spec(SMEM)] * 7 + [spec(VMEM)] * 3,
        out_specs=[spec(VMEM)] * 2,
        compiler_params=PARAMS,
        name="place",
    )(target, neighbours, *constants, boxes, first, second)
    state, *planes = pl.pallas_call(
        place_y_kernel,
        out_shape=[struct(ROWS, 128)] + PLANES,
        in_specs=[spec(VMEM), spec(pl.ANY)],
        out_specs=[spec(VMEM)] * 5,
        input_output_aliases={0: 0},
        scratch_shapes=[
            VMEM((count_y, TAG, 128), F32),
            pltpu.SemaphoreType.DMA,
            pltpu.SemaphoreType.DMA((SLOTS,)),
        ],
        compiler_params=PARAMS,
        name="place_y",
    )(state, all_y)
    for step_index in range(STEPS):
        x_a, x_b, y_a, y_b = planes
        received = (swapped(x_a, "gx", 0), swapped(x_b, "gx", 1), swapped(y_a, "gy", 0), swapped(y_b, "gy", 1))
        part = inside(table, state)
        if step_index < STEPS - 1:
            state, *planes = add_ghosts(False, table, part, planes, received)
        else:
            state = add_ghosts(True, table, part, planes, received)
    return state.reshape(COMPS, 128, SLOTS, 128).transpose(2, 0, 1, 3).reshape(SLOTS, COMPS, BZ * BX * BX)


def solution(mesh):
    return jax.shard_map(
        shards,
        mesh=mesh,
        in_specs=(
            P(("gx", "gy"), None, None),
            P(("gx", "gy")),
            P(("gx", "gy")),
            P(("gx", "gy"), None),
            P(),
            P(),
            P(),
            P(),
            P(),
        ),
        out_specs=P(("gx", "gy"), None, None),
        check_vma=False,
    )
```
